32 devices in a mesh: tm: 8 (over z, x), chan: 4 (over y, core).
Axes of the slice: x: 2, y: 2, z: 4, core: 2. Of those that a mesh axis runs over, the one named last changes fastest.
Arguments:
- fwd_in: bfloat16 [16384, 512], P('tm', 'chan'), may hold values from -28 to 28, as said below
- bwd_in: bfloat16 [16384, 512], P('tm', 'chan'), may hold values from -28 to 28, as said below
Outputs:
- forward_error: bfloat16 [16384, 512], P('tm', 'chan')
- backward_error: bfloat16 [16384, 512], P('tm', 'chan')
The draws below stay inside these ranges and needn't reach their ends.
Inputs may be any that keep to these rules, and one draw needn't show every extreme that they name: `fwd_in`: real-valued samples. `bwd_in`: real-valued samples.
All inputs are finite; a program needn't handle non-finite values.
Results may differ from the reference program's by a relative error of at most 0.0066.
Values may be sent and summed in bfloat16 or wider, within the bound.
No kernel may reach another device: no remote copies, remote signals or barrier semaphores. Data moves between devices by JAX's collectives and lax.ppermute only.
A program may use at most 64 MiB of HBM per device.

```python
import math
import jax
import jax.numpy as jnp
from jax import lax

C = 512
TD = 2048
ORDERS = 2
NSTEPS = 6
SAMPLES = 16384


def error_pair(key):
    keys = jax.random.split(jax.random.fold_in(key, 17), 13)
    seg_rows = TD // 4
    seg_count = SAMPLES // seg_rows
    factor_series = jnp.clip(jax.random.normal(keys[10], (SAMPLES + 1, 3), jnp.float32), -4.0, 4.0)
    loadings = 0.15 * jax.random.normal(keys[11], (3, C), jnp.float32)
    shared = factor_series[:, 0:1] * loadings[0:1] + factor_series[:, 1:2] * loadings[1:2] + factor_series[:, 2:3] * loadings[2:3]
    lead = jnp.clip(jax.random.normal(keys[0], (SAMPLES + 1, C), jnp.float32), -4.0, 4.0) + shared
    own = 0.3 * jnp.clip(jax.random.normal(keys[1], (SAMPLES, C), jnp.float32), -4.0, 4.0)
    block_scale = jnp.exp(jax.random.uniform(keys[4], (seg_count, 1), jnp.float32, 0.0, math.log(10.0)))
    mix_sign = jnp.where(jax.random.uniform(keys[12], (), jnp.float32) < 0.5, -1.0, 1.0)
    block_mix = mix_sign * jax.random.uniform(keys[5], (seg_count, 1), jnp.float32, 0.6, 0.9)
    scale_rows = jnp.repeat(block_scale, seg_rows, axis=0)
    mix_rows = jnp.repeat(block_mix, seg_rows, axis=0)
    current = lead[:-1]
    earlier = jnp.concatenate([jnp.zeros((1, C), jnp.float32), current[:-1]], axis=0)
    base_fwd = current + 0.5 * earlier
    own_before = jnp.concatenate([jnp.zeros((1, C), jnp.float32), own[:-1]], axis=0)
    base_bwd = own + mix_rows * lead[1:] - 0.4 * own_before
    scale_fwd = jnp.exp(jax.random.uniform(keys[2], (1, C), jnp.float32, 0.0, math.log(3.2)))
    scale_bwd = jnp.exp(jax.random.uniform(keys[3], (1, C), jnp.float32, 0.0, math.log(3.2)))
    jitter_fwd = jnp.exp(jax.random.uniform(keys[8], (SAMPLES, 1), jnp.float32, 0.0, math.log(1.6)))
    jitter_bwd = jnp.exp(jax.random.uniform(keys[9], (SAMPLES, 1), jnp.float32, 0.0, math.log(1.6)))
    first = jnp.clip(base_fwd * scale_fwd * scale_rows * jitter_fwd / 6.0, -27.0, 27.0)
    second = jnp.clip(base_bwd * scale_bwd * scale_rows * jitter_bwd / 6.0, -27.0, 27.0)
    return (first, second)


def draw_fwd_in(key, part):
    first, second = error_pair(key)
    return first.astype(jnp.bfloat16)


def draw_bwd_in(key, part):
    first, second = error_pair(key)
    return second.astype(jnp.bfloat16)


def setup_inputs(seed: int = 0) -> dict:
    arg_keys = jax.random.split(jax.random.key(seed), 3)
    fwd_in = draw_fwd_in(jax.random.fold_in(arg_keys[2], 71), 0)
    bwd_in = draw_bwd_in(jax.random.fold_in(arg_keys[2], 71), 0)
    return {"fwd_in": fwd_in, "bwd_in": bwd_in}


def covariance(left, right):
    return jnp.dot(left.astype(jnp.float32).T, right.astype(jnp.float32), precision=lax.Precision.HIGHEST)

def newton_inverse(matrix):
    factor = lax.rsqrt(jnp.sum(matrix * matrix) + 1e-06)
    iterate = factor * jnp.eye(C, dtype=jnp.float32)
    for step in range(NSTEPS):
        product = jnp.dot(matrix, iterate, precision=lax.Precision.HIGHEST)
        iterate = 2.0 * iterate - jnp.dot(product, iterate, precision=lax.Precision.HIGHEST)
    return iterate

def reference(fwd_in, bwd_in):
    forward = fwd_in
    backward = bwd_in
    for order in range(ORDERS):
        shifted = jnp.concatenate([jnp.zeros((1, C), jnp.bfloat16), backward[:-1]], axis=0)
        cov_fwd = covariance(forward, forward)
        cov_bwd = covariance(shifted, shifted)
        cov_cross = covariance(forward, shifted)
        inv_fwd = newton_inverse(cov_fwd)
        inv_bwd = newton_inverse(cov_bwd)
        refl_fwd = (-jnp.dot(cov_cross, inv_bwd, precision=lax.Precision.HIGHEST)).astype(jnp.bfloat16)
        refl_bwd = (-jnp.dot(cov_cross.T, inv_fwd, precision=lax.Precision.HIGHEST)).astype(jnp.bfloat16)
        new_forward = forward.astype(jnp.float32) + jnp.dot(shifted.astype(jnp.float32), refl_fwd.astype(jnp.float32).T, precision=lax.Precision.HIGHEST)
        new_backward = shifted.astype(jnp.float32) + jnp.dot(forward.astype(jnp.float32), refl_bwd.astype(jnp.float32).T, precision=lax.Precision.HIGHEST)
        forward = new_forward.astype(jnp.bfloat16)
        backward = new_backward.astype(jnp.bfloat16)
    return (forward, backward)
```

```python
import jax
import jax.numpy as jnp
from jax import lax
from jax.sharding import Mesh, PartitionSpec as P

ORDERS = 2
NSTEPS = 6
HIGH = lax.Precision.HIGH
F32 = jnp.float32
BF16 = jnp.bfloat16
PARTS = ("z", "x", "y")
LANES = 128


def swap(value, axis):
    return lax.ppermute(value, axis, [(0, 1), (1, 0)])


def from_behind(value, axes):
    devices = lax.axis_size(axes)
    return lax.ppermute(value, axes, [(i, i + 1) for i in range(devices - 1)])


def ring_gather(piece, axis):
    size = lax.axis_size(axis)
    me = lax.axis_index(axis)
    out = jnp.zeros((size,) + piece.shape, piece.dtype)
    out = lax.dynamic_update_index_in_dim(out, piece, me, 0)
    for by in range(1, size):
        got = lax.ppermute(piece, axis, [(i, (i + by) % size) for i in range(size)])
        out = lax.dynamic_update_index_in_dim(out, got, lax.rem(me - by + size, size), 0)
    return out


def xy_gather(piece):
    x, y = lax.axis_index("x"), lax.axis_index("y")
    both = lax.ppermute(piece, ("x", "y"), [(i, 3 - i) for i in range(4)])
    pieces = (piece, swap(piece, "y"), swap(piece, "x"), both)
    out = jnp.zeros((4,) + piece.shape, piece.dtype)
    for i, value in enumerate(pieces):
        out = lax.dynamic_update_index_in_dim(out, value, (x * 2 + y) ^ i, 0)
    return out


def total(partial):
    shape = partial.shape
    parts = lax.axis_size(PARTS)
    cut = partial.reshape(parts, -1, LANES)
    mine = jnp.sum(lax.all_to_all(cut, PARTS, 0, 0, tiled=True), axis=0)
    column = ring_gather(mine, "z")
    whole = xy_gather(column)
    return jnp.swapaxes(whole, 0, 1).reshape(shape)


def gram(left, right):
    return lax.dot_general(left, right, (((0,), (0,)), ((), ())), preferred_element_type=F32)


def symmetric_total(samples, width):
    blocks = samples.shape[1] // width
    rows = [gram(samples[:, i * width : (i + 1) * width], samples[:, i * width :]) for i in range(blocks)]
    packed = total(jnp.concatenate([r[:, j * width : (j + 1) * width] for i, r in enumerate(rows) for j in range(blocks - i)], axis=0))
    table, k = {}, 0
    for i in range(blocks):
        for j in range(i, blocks):
            table[i, j] = packed[k * width : (k + 1) * width]
            table[j, i] = table[i, j].T
            k += 1
    return jnp.concatenate(
        [jnp.concatenate([table[i, j] for j in range(blocks)], axis=1) for i in range(blocks)], axis=0
    )


def inverse(matrix):
    factor = lax.rsqrt(jnp.sum(matrix * matrix) + 1e-06)
    error = factor * matrix
    iterate = 2.0 * jnp.eye(matrix.shape[0], dtype=F32) - error
    for step in range(1, NSTEPS):
        error = 2.0 * error - jnp.dot(error, error, precision=HIGH)
        iterate = 2.0 * iterate - jnp.dot(error, iterate, precision=HIGH)
    return factor * iterate


def local(fwd_in, bwd_in):
    y, core = lax.axis_index("y"), lax.axis_index("core")
    samples, own = fwd_in.shape
    half = samples // 2
    both = jnp.stack([fwd_in, bwd_in])
    mine = lax.dynamic_slice_in_dim(both, y * half, half, 1)
    other = lax.dynamic_slice_in_dim(both, (1 - y) * half, half, 1)

    def channels(own, across):
        pair = jnp.where(y == 0, jnp.stack([own, across]), jnp.stack([across, own]))
        beside = swap(pair, "core")
        lo, hi = jnp.where(core == 0, pair, beside), jnp.where(core == 0, beside, pair)
        return jnp.concatenate([lo[0], hi[0], lo[1], hi[1]], axis=-1)

    here = channels(mine, swap(other, "y"))
    there = channels(other, swap(mine, "y"))
    near = jnp.where(y == 0, here, there)
    far = jnp.where(y == 0, there, here)
    whole = jnp.concatenate([near, far], axis=1)
    forward, backward = whole[0], whole[1]
    last = lax.axis_index(PARTS) == lax.axis_size(PARTS) - 1
    row = lax.broadcasted_iota(jnp.int32, (half, 1), 0)
    width = forward.shape[1] // 2
    first, second = here[0], here[1]
    for order in range(ORDERS):
        before = from_behind(backward[-1:], ("z", "x"))
        shifted = jnp.concatenate([before, backward[:-1]], axis=0)
        kept = jnp.where(last & (row == half - 1), jnp.zeros((), BF16), second)
        cov = symmetric_total(jnp.where(core == 0, first, kept), own)
        delayed = lax.dynamic_slice_in_dim(shifted, y * half, half, 0)
        cross = total(gram(lax.dynamic_slice_in_dim(first, core * width, width, 1), delayed))
        beside = swap(cross, "core")
        cross = jnp.where(core == 0, jnp.concatenate([cross, beside]), jnp.concatenate([beside, cross]))
        inv = inverse(cov)
        refl = (-jnp.dot(jnp.where(core == 1, cross, cross.T), inv, precision=HIGH)).astype(BF16)
        refl_other = swap(refl, "core")
        refl_fwd = jnp.where(core == 1, refl, refl_other)
        refl_bwd = jnp.where(core == 1, refl_other, refl)
        keep_fwd, keep_bwd = forward, shifted
        if order == ORDERS - 1:
            start = (y * 2 + core) * own
            refl_fwd = lax.dynamic_slice_in_dim(refl_fwd, start, own, 0)
            refl_bwd = lax.dynamic_slice_in_dim(refl_bwd, start, own, 0)
            keep_fwd = lax.dynamic_slice_in_dim(forward, start, own, 1)
            keep_bwd = lax.dynamic_slice_in_dim(shifted, start, own, 1)
        new_forward = keep_fwd.astype(F32) + lax.dot_general(
            shifted, refl_fwd, (((1,), (1,)), ((), ())), preferred_element_type=F32
        )
        new_backward = keep_bwd.astype(F32) + lax.dot_general(
            forward, refl_bwd, (((1,), (1,)), ((), ())), preferred_element_type=F32
        )
        forward = new_forward.astype(BF16)
        backward = new_backward.astype(BF16)
        if order < ORDERS - 1:
            first = lax.dynamic_slice_in_dim(forward, y * half, half, 0)
            second = lax.dynamic_slice_in_dim(backward, y * half, half, 0)
    return forward, backward


def solution(mesh):
    tm, chan = mesh.shape["tm"], mesh.shape["chan"]
    split = Mesh(mesh.devices.reshape(tm // 2, 2, chan // 2, 2), ("z", "x", "y", "core"))
    spec = P(("z", "x"), ("y", "core"))
    return jax.shard_map(local, mesh=split, in_specs=(spec, spec), out_specs=(spec, spec), check_vma=False)
```

```python
import functools

import jax
import jax.numpy as jnp
from jax import lax
from jax.experimental import pallas as pl
from jax.experimental.pallas import tpu as pltpu
from jax.sharding import Mesh, PartitionSpec as P

ORDERS = 2
NSTEPS = 6
F32 = jnp.float32
BF16 = jnp.bfloat16
PARTS = ("z", "x", "y")
LANES = 128
VMEM = pl.BlockSpec(memory_space=pltpu.VMEM)


def swap(value, axis):
    return lax.ppermute(value, axis, [(0, 1), (1, 0)])


def from_behind(value, axes):
    devices = lax.axis_size(axes)
    return lax.ppermute(value, axes, [(i, i + 1) for i in range(devices - 1)])


def after(value, *others):
    return lax.optimization_barrier((value,) + others)[0]


def call(body, shapes, scratch, flops, *args):
    size = sum(a.size * a.dtype.itemsize for a in args) + sum(s.size * s.dtype.itemsize for s in shapes)
    return pl.pallas_call(
        body,
        out_shape=shapes,
        in_specs=[VMEM] * len(args),
        out_specs=[VMEM] * len(shapes),
        scratch_shapes=scratch,
        compiler_params=pltpu.CompilerParams(vmem_limit_bytes=32 << 20),
        cost_estimate=pl.CostEstimate(flops=flops, bytes_accessed=size, transcendentals=0),
    )(*args)


def place():
    return lax.axis_index("z"), lax.axis_index("x") * 2 + lax.axis_index("y"), lax.axis_index("core")


def dot(a, b):
    return jnp.dot(a, b, preferred_element_type=F32)


def dot_first(a, b):
    return lax.dot_general(a, b, (((0,), (0,)), ((), ())), preferred_element_type=F32)


def dot_last(a, b):
    return lax.dot_general(a, b, (((1,), (1,)), ((), ())), preferred_element_type=F32)


def halves(value):
    high = value.astype(BF16)
    return high, (value - high.astype(F32)).astype(BF16)


def assemble(pieces, out, width):
    y, core = lax.axis_index("y"), lax.axis_index("core")
    for i, piece in enumerate(pieces):
        block = (y ^ (i & 1)) * 2 + (core ^ (i >> 1))
        out[:, :, pl.ds(pl.multiple_of(block * width, LANES), width)] = piece[...]


def delay(source, before, out):
    rows = source.shape[0]
    step = min(rows, 256)
    top = lax.broadcasted_iota(jnp.int32, (step, 1), 0) == 0
    for r in range(0, rows, step):
        edge = (before[...] if r == 0 else source[r - 16 : r]).astype(F32)[15:16]
        moved = pltpu.roll(source[r : r + step].astype(F32), 1, 0)
        out[r : r + step] = jnp.where(top, edge, moved).astype(BF16)


def pack_gram(samples, packed, width):
    blocks = samples.shape[1] // width
    k, rows = 0, {}
    for i in range(0, blocks, 2):
        value = dot_first(samples[:, i * width : (i + 2) * width], samples[:, i * width :])
        rows[i], rows[i + 1] = (i, value[:width]), (i, value[width:])
    for i in range(blocks):
        start, value = rows[i]
        for j in range(i, blocks):
            packed[k * width : (k + 1) * width] = value[:, (j - start) * width : (j - start + 1) * width]
            k += 1
    if packed.shape[0] > k * width:
        packed[k * width :] = jnp.zeros((packed.shape[0] - k * width, LANES), F32)


def own_gram(here, samples, packed, width):
    core = lax.axis_index("core")
    samples[...] = here[core]
    rows = samples.shape[0]

    @pl.when((core == 1) & (lax.axis_index(PARTS) == lax.axis_size(PARTS) - 1))
    def _():
        tail = samples[rows - 16 :].astype(F32)
        inside = lax.broadcasted_iota(jnp.int32, (16, 1), 0) < 15
        samples[rows - 16 :] = jnp.where(inside, tail, 0.0).astype(BF16)

    pack_gram(samples, packed, width)


def unpack(pieces, out, base=0):
    z, xy, _ = place()
    for i, piece in enumerate(pieces):
        depth, rows = piece.shape[0], piece.shape[1]
        for k in range(depth):
            part = lax.rem(z + depth - k, depth) * 4 + (xy ^ i)
            out[pl.ds(pl.multiple_of(base + part * rows, 8), rows)] = piece[k]


def first_kernel(width, *refs):
    pieces, (here, packed, samples) = refs[:4], refs[4:]
    assemble(pieces, here, width)
    own_gram(here, samples, packed, width)


def cross_kernel(width, here, before, shifted, packed):
    core = lax.axis_index("core")
    delay(here.at[1], before, shifted)
    channels = here.shape[2]
    half = channels // 2
    value = dot_first(here[0, :, pl.ds(pl.multiple_of(core * half, LANES), half)], shifted[...])
    for j in range(channels // LANES):
        packed[j * half : (j + 1) * half] = value[:, j * LANES : (j + 1) * LANES]
    used = half * channels // LANES
    if packed.shape[0] > used:
        packed[used:] = jnp.zeros((packed.shape[0] - used, LANES), F32)


def gather_kernel(width, *refs):
    pieces, before, here, shifted = refs[:4], refs[4], refs[5], refs[6]
    assemble(pieces, here, width)
    delay(here.at[1], before, shifted)


def inverse_kernel(width, *refs):
    pieces, out, packed = refs[:4], refs[4], refs[5]
    errors, highs, lows, its, ihighs, ilows = refs[6:]
    unpack(pieces, packed)
    channels = out.shape[0]
    blocks = channels // width
    k, norm = 0, jnp.zeros((8, LANES), F32)
    for i in range(blocks):
        for j in range(i, blocks):
            block = packed[k * width : (k + 1) * width]
            squares = jnp.sum((block * block).reshape(-1, 8, LANES), axis=0)
            norm = norm + (squares if i == j else 2.0 * squares)
            k += 1
    factor = lax.rsqrt(jnp.sum(norm, keepdims=True) + 1e-06)
    eye = lax.broadcasted_iota(jnp.int32, (width, width), 0) == lax.broadcasted_iota(jnp.int32, (width, width), 1)

    def put(table, high, low, slot, rows, cols, value):
        table[slot, rows, cols] = value
        high[slot, rows, cols], low[slot, rows, cols] = halves(value)

    k = 0
    for i in range(blocks):
        for j in range(i, blocks):
            value = packed[k * width : (k + 1) * width] * factor
            k += 1
            for a, b, v in ((i, j, value),) + (() if i == j else ((j, i, value.T),)):
                rows, cols = pl.ds(a * width, width), pl.ds(b * width, width)
                put(errors, highs, lows, 0, rows, cols, v)
                put(its, ihighs, ilows, 1, rows, cols, jnp.where(eye, 2.0, 0.0) - v if a == b else -v)
    step = channels // 2
    every = pl.ds(0, channels)
    for n in range(NSTEPS):
        now, later = n % 2, (n + 1) % 2
        for r in range(0, channels, step):
            rows = pl.ds(r, step)
            high, low = highs[now, rows], lows[now, rows]
            if n < NSTEPS - 1:
                value = dot(high, highs[now]) + dot(high, lows[now]) + dot(low, highs[now])
                put(errors, highs, lows, later, rows, every, 2.0 * errors[now, rows] - value)
            if n >= 1:
                value = dot(high, ihighs[now]) + dot(high, ilows[now]) + dot(low, ihighs[now])
                value = 2.0 * its[now, rows] - value
                if n < NSTEPS - 1:
                    put(its, ihighs, ilows, later, rows, every, value)
                else:
                    out[rows] = value * factor


def reflect_kernel(*refs):
    ours, theirs, inv, out = refs[:4], refs[4], refs[5], refs[6]
    packed, high, low, ihigh, ilow = refs[7:]
    core = lax.axis_index("core")
    channels = out.shape[0]
    half = channels // 2

    def fill(start):
        rows = pl.ds(pl.multiple_of(start, 16), half)
        for j in range(channels // LANES):
            cols = pl.ds(j * LANES, LANES)
            high[rows, cols], low[rows, cols] = halves(packed[j * half : (j + 1) * half])

    unpack(ours, packed)
    fill(core * half)
    unpack([theirs.at[i] for i in range(4)], packed)
    fill((1 - core) * half)
    ihigh[...], ilow[...] = halves(inv[...])
    for chosen, product in ((0, dot_first), (1, dot)):

        @pl.when(core == chosen)
        def _():
            value = product(high[...], ihigh[...]) + product(high[...], ilow[...]) + product(low[...], ihigh[...])
            out[...] = (-value).astype(BF16)


def update(here, shifted, refl, out, rows):
    forward, backward = here[0, rows], shifted[rows]
    out[0, rows] = (forward.astype(F32) + dot_last(backward, refl[0])).astype(BF16)
    out[1, rows] = (backward.astype(F32) + dot_last(forward, refl[1])).astype(BF16)


def by_kind(ours, theirs, refl):
    core = lax.axis_index("core")
    refl[1 - core] = ours[...]
    refl[core] = theirs[...]


def update_gram_kernel(width, here, shifted, ours, theirs, out, packed, refl, samples):
    by_kind(ours, theirs, refl)
    step = 256
    for r in range(0, here.shape[1], step):
        update(here, shifted, refl, out, slice(r, r + step))
    own_gram(out, samples, packed, width)


def update_delay_kernel(here, shifted, ours, theirs, before, ours_tail, out, later, refl, edge):
    by_kind(ours, theirs, refl)
    step = 256
    for r in range(0, here.shape[1], step):
        update(here, shifted, refl, out, slice(r, r + step))
    y = lax.axis_index("y")
    edge[0] = ours_tail[...]
    edge[1] = before[...]
    delay(out.at[1], edge.at[y], later)


def last_kernel(width, here, shifted, there, there_shifted, ours, theirs, forward, backward, refl):
    y, core = lax.axis_index("y"), lax.axis_index("core")
    by_kind(ours, theirs, refl)
    mine = pl.multiple_of((y * 2 + core) * width, LANES)
    half = here.shape[1]
    left, right = refl[0, pl.ds(mine, width)], refl[1, pl.ds(mine, width)]
    for time, (both, late) in ((y, (here, shifted)), (1 - y, (there, there_shifted))):
        rows = pl.ds(pl.multiple_of(time * half, 16), half)
        cols = pl.ds(mine, width)
        forward[rows] = (both[0, :, cols].astype(F32) + dot_last(late[...], left)).astype(BF16)
        backward[rows] = (late[:, cols].astype(F32) + dot_last(both[0], right)).astype(BF16)


def scatter_sum(packed):
    parts = lax.axis_size(PARTS)
    cut = packed.reshape(parts, -1, LANES)
    return jnp.sum(lax.all_to_all(cut, PARTS, 0, 0, tiled=True), axis=0)


def z_gather(piece):
    size = lax.axis_size("z")
    shift = lambda by: [(i, (i + by) % size) for i in range(size)]
    return jnp.stack([piece] + [lax.ppermute(piece, "z", shift(by)) for by in range(1, size)])


def xy_gather(piece):
    return [
        piece,
        swap(piece, "y"),
        swap(piece, "x"),
        lax.ppermute(piece, ("x", "y"), [(i, 3 - i) for i in range(4)]),
    ]


def rounded(rows, parts):
    return -(-rows // (8 * parts)) * 8 * parts


def local(fwd_in, bwd_in):
    y = lax.axis_index("y")
    samples, width = fwd_in.shape
    half = samples // 2
    channels = width * 4
    parts = lax.axis_size(PARTS)
    blocks = channels // width
    sym_rows = rounded(blocks * (blocks + 1) // 2 * width, parts)
    cross_rows = rounded(channels // 2 * channels // LANES, parts)
    both = jnp.stack([fwd_in, bwd_in])
    mine = lax.dynamic_slice_in_dim(both, y * half, half, 1)
    other = lax.dynamic_slice_in_dim(both, (1 - y) * half, half, 1)
    square = lambda *lead: pltpu.VMEM(lead + (channels, channels), F32)
    square16 = lambda *lead: pltpu.VMEM(lead + (channels, channels), BF16)
    shape = jax.ShapeDtypeStruct

    across = swap(other, "y")
    mine_core = swap(mine, "core")
    across_core = swap(across, "core")
    here, packed = call(
        functools.partial(first_kernel, width),
        [shape((2, half, channels), BF16), shape((sym_rows, LANES), F32)],
        [pltpu.VMEM((half, channels), BF16)],
        2 * half * channels * channels,
        mine, across, mine_core, across_core,
    )
    there = there_shifted = None
    for order in range(ORDERS):
        before = from_behind(here[1, half - 16 :], PARTS)
        before_z = from_behind(here[1, half - 16 :], ("z", "x"))
        column = z_gather(scatter_sum(packed))
        pieces = xy_gather(column)
        shifted, cross = call(
            functools.partial(cross_kernel, width),
            [shape((half, channels), BF16), shape((cross_rows, LANES), F32)],
            [],
            half * channels * channels,
            here, before,
        )
        cross_column = z_gather(scatter_sum(cross))
        ours = xy_gather(cross_column)
        theirs = swap(jnp.stack(ours), "core")
        (inv,) = call(
            functools.partial(inverse_kernel, width),
            [shape((channels, channels), F32)],
            [pltpu.VMEM((sym_rows, LANES), F32)] + [square(2), square16(2), square16(2)] * 2,
            60 * channels**3,
            *pieces,
        )
        (refl,) = call(
            reflect_kernel,
            [shape((channels, channels), BF16)],
            [pltpu.VMEM((cross_rows, LANES), F32)] + [square16()] * 4,
            6 * channels**3,
            *ours, theirs, inv,
        )
        refl_core = swap(refl, "core")
        if order == 0:
            late = after(mine, column)
            across2 = swap(late, "y")
            other_core = swap(other, "core")
            across2_core = swap(across2, "core")
            edge = jnp.where(y == 0, here[1, half - 16 :], before_z)
            there, there_shifted = call(
                functools.partial(gather_kernel, width),
                [shape((2, half, channels), BF16), shape((half, channels), BF16)],
                [],
                0,
                other, across2, other_core, across2_core, edge,
            )
        if order < ORDERS - 1:
            here_new, packed = call(
                functools.partial(update_gram_kernel, width),
                [shape((2, half, channels), BF16), shape((sym_rows, LANES), F32)],
                [square16(2), pltpu.VMEM((half, channels), BF16)],
                6 * half * channels * channels,
                here, shifted, refl, refl_core,
            )
            tail = here_new[1, half - 16 :]
            there, there_shifted = call(
                update_delay_kernel,
                [shape((2, half, channels), BF16), shape((half, channels), BF16)],
                [square16(2), pltpu.VMEM((2, 16, channels), BF16)],
                4 * half * channels * channels,
                there, there_shifted, refl, refl_core, from_behind(tail, ("z", "x")), tail,
            )
            here = here_new
    forward, backward = call(
        functools.partial(last_kernel, width),
        [shape((samples, width), BF16)] * 2,
        [square16(2)],
        4 * samples * channels * width,
        here, shifted, there, there_shifted, refl, refl_core,
    )
    return forward, backward


def solution(mesh):
    tm, chan = mesh.shape["tm"], mesh.shape["chan"]
    split = Mesh(mesh.devices.reshape(tm // 2, 2, chan // 2, 2), ("z", "x", "y", "core"))
    spec = P(("z", "x"), ("y", "core"))
    return jax.shard_map(local, mesh=split, in_specs=(spec, spec), out_specs=(spec, spec), check_vma=False)
```

```python
import functools

import jax
import jax.numpy as jnp
from jax import lax
from jax.experimental import pallas as pl
from jax.experimental.pallas import tpu as pltpu
from jax.sharding import Mesh, PartitionSpec as P

ORDERS = 2
NSTEPS = 6
F32 = jnp.float32
BF16 = jnp.bfloat16
PARTS = ("z", "x", "y")
LANES = 128
VMEM = pl.BlockSpec(memory_space=pltpu.VMEM)


def swap(value, axis):
    return lax.ppermute(value, axis, [(0, 1), (1, 0)])


def from_behind(value, axes):
    devices = lax.axis_size(axes)
    return lax.ppermute(value, axes, [(i, i + 1) for i in range(devices - 1)])


def after(value, *others):
    return lax.optimization_barrier((value,) + others)[0]


def call(body, shapes, scratch, flops, *args):
    size = sum(a.size * a.dtype.itemsize for a in args) + sum(s.size * s.dtype.itemsize for s in shapes)
    return pl.pallas_call(
        body,
        out_shape=shapes,
        in_specs=[VMEM] * len(args),
        out_specs=[VMEM] * len(shapes),
        scratch_shapes=scratch,
        compiler_params=pltpu.CompilerParams(vmem_limit_bytes=16 << 20),
        cost_estimate=pl.CostEstimate(flops=flops, bytes_accessed=size, transcendentals=0),
    )(*args)


def dot(a, b):
    return jnp.dot(a, b, preferred_element_type=F32)


def dot_first(a, b):
    return lax.dot_general(a, b, (((0,), (0,)), ((), ())), preferred_element_type=F32)


def dot_last(a, b):
    return lax.dot_general(a, b, (((1,), (1,)), ((), ())), preferred_element_type=F32)


def halves(value):
    high = value.astype(BF16)
    return high, (value - high.astype(F32)).astype(BF16)


def thirds(value):
    high, rest = value.astype(BF16), value - value.astype(BF16).astype(F32)
    return (high,) + halves(rest)


def at(index, size):
    return pl.ds(pl.multiple_of(index * size, size), size)


def delay(source, before, out):
    rows = source.shape[0]
    step = min(rows, 256)
    top = lax.broadcasted_iota(jnp.int32, (step, 1), 0) == 0
    for r in range(0, rows, step):
        edge = (before[...] if r == 0 else source[r - 16 : r]).astype(F32)[15:16]
        moved = pltpu.roll(source[r : r + step].astype(F32), 1, 0)
        out[r : r + step] = jnp.where(top, edge, moved).astype(BF16)


def drop_end(samples, here):
    rows = samples.shape[0]

    @pl.when((lax.axis_index("core") == 1) & here)
    def _():
        tail = samples[rows - 16 :].astype(F32)
        inside = lax.broadcasted_iota(jnp.int32, (16, 1), 0) < 15
        samples[rows - 16 :] = jnp.where(inside, tail, 0.0).astype(BF16)


def emit(blocks, flat, outs, start, each):
    used = 0
    for block in blocks:
        flat[used : used + block.shape[0]] = block
        used += block.shape[0]
    depth = outs[0].shape[0]
    parts = depth * len(outs)
    if parts * each > used:
        flat[used : parts * each] = jnp.zeros((parts * each - used, LANES), F32)
    z, x, y = lax.axis_index("z"), lax.axis_index("x"), lax.axis_index("y")
    for i, out in enumerate(outs):
        for k in range(depth):
            part = lax.rem(z + k, depth) * len(outs) + ((x * 2 + y if len(outs) == 4 else x) ^ i)
            out[k, start : start + each] = flat[at(part, each)]


def sources(depth):
    z, x, y = lax.axis_index("z"), lax.axis_index("x"), lax.axis_index("y")
    for i in range(4):
        for k in range(depth):
            xs, ys = x ^ (i >> 1), y ^ (i & 1)
            zx = lax.rem(z + depth - k, depth) * 2 + xs
            yield i, k, zx, ys


def gather_blocks(piece, depth, start, near_each, far_each, near, far):
    for i, k, zx, ys in sources(depth):
        near[ys, at(zx, near_each)] = piece(i)[k, start : start + near_each]
        far[at(zx * 2 + ys, far_each)] = piece(i)[k, start + near_each : start + near_each + far_each]


def steps(first, last, errors, highs, lows, its, ihighs, ilows, finish):
    channels = errors.shape[1]
    step = channels // 2
    for n in range(first, last):
        now, later = n % 2, (n + 1) % 2
        for r in range(0, channels, step):
            rows = pl.ds(r, step)
            high, low = highs[now, rows], lows[now, rows]
            if n < NSTEPS - 1:
                value = dot(high, highs[now]) + dot(high, lows[now]) + dot(low, highs[now])
                value = 2.0 * errors[now, rows] - value
                errors[later, rows] = value
                highs[later, rows], lows[later, rows] = halves(value)
            if n >= 1:
                value = dot(high, ihighs[now]) + dot(high, ilows[now]) + dot(low, ihighs[now])
                value = 2.0 * its[now, rows] - value
                if n == NSTEPS - 1:
                    finish(rows, value)
                else:
                    its[later, rows] = value
                    ihighs[later, rows], ilows[later, rows] = halves(value)


def put(table, high, low, slot, rows, cols, value):
    table[slot, rows, cols] = value
    high[slot, rows, cols], low[slot, rows, cols] = halves(value)


def by_kind(ours, theirs, refl):
    core = lax.axis_index("core")
    refl[1 - core] = ours[...]
    refl[core] = theirs[...]


def update(both, shifted, refl, out):
    step = 256
    for r in range(0, both.shape[1], step):
        rows = slice(r, r + step)
        forward, backward = both[0, rows], shifted[rows]
        out[0, rows] = (forward.astype(F32) + dot_last(backward, refl[0])).astype(BF16)
        out[1, rows] = (backward.astype(F32) + dot_last(forward, refl[1])).astype(BF16)


def update_edge(edge, refl, out):
    late = pltpu.roll(edge[1].astype(F32), 1, 0)
    out[...] = (late + dot_last(edge[0], refl[1])).astype(BF16)


def near_kernel(width, pd, xd, both, both_core, halo, halo_core, *refs):
    packed, (chosen, behind, late, edge, flat) = refs[:2], refs[2:]
    core = lax.axis_index("core")
    own, other = at(core, width), at(1 - core, width)
    chosen[:, own], chosen[:, other] = both[core], both_core[core]
    behind[:, own], behind[:, other] = both[1], both_core[1]
    edge[:, own], edge[:, other] = halo[1], halo_core[1]
    zx = ("z", "x")
    drop_end(chosen, lax.axis_index(zx) == lax.axis_size(zx) - 1)
    value = dot_first(chosen[...], chosen[...])
    emit([value[:width, :width], value[:width, width:], value[width:, width:]], flat, packed, 0, pd)
    delay(behind, edge, late)
    value = dot_first(both[0], late[...])
    emit([value[:, :width], value[:, width:]], flat, packed, pd, xd)


def far_kernel(width, po, xo, both, across, both_core, across_core, halo, halo_core, halo_y, halo_y_core, *refs):
    (here, edge, shifted), packed, (tails, samples, flat) = refs[:3], refs[3:7], refs[7:]
    y, core = lax.axis_index("y"), lax.axis_index("core")
    half = here.shape[1]
    pair = 2 * width
    mine, beside = at(y * 2 + core, width), at(y * 2 + 1 - core, width)
    over, over_beside = at((1 - y) * 2 + core, width), at((1 - y) * 2 + 1 - core, width)
    rows = at(y, half)
    here[:, :, mine], here[:, :, beside] = both[:, rows], both_core[:, rows]
    here[:, :, over], here[:, :, over_beside] = across[...], across_core[...]
    edge[:, :, over], edge[:, :, over_beside] = halo_y[...], halo_y_core[...]

    @pl.when(y == 0)
    def _():
        edge[:, :, mine], edge[:, :, beside] = halo[...], halo_core[...]

    @pl.when(y == 1)
    def _():
        edge[:, :, mine], edge[:, :, beside] = both[:, half - 16 : half], both_core[:, half - 16 : half]

    samples[...] = here[core]
    drop_end(samples, lax.axis_index(PARTS) == lax.axis_size(PARTS) - 1)
    value = dot_first(samples[:, :pair], samples[:, pair:])
    blocks = lambda v: [v[i : i + width, j : j + width] for i in (0, width) for j in (0, width)]
    emit(blocks(value), flat, packed, 0, po)
    delay(here.at[1], edge.at[1], shifted)
    value = dot_first(here[0, :, at(core, pair)], shifted[:, at(1 - core, pair)])
    emit(blocks(value), flat, packed, po, xo)
    for i, rows in enumerate((here[0, half - 16 :], shifted[half - 16 :])):
        row = rows.astype(F32)[15:16]
        for j in range(4):
            tails[i * 4 + j : i * 4 + j + 1] = row[:, j * LANES : (j + 1) * LANES]


def inverse_kernel(width, pd, po, stop, *refs):
    pieces, (full, error, iterate, scale), (near, far) = refs[:4], refs[4:8], refs[8:10]
    tables = refs[10:]
    errors, highs, lows, its, ihighs, ilows = tables
    gather_blocks(lambda i: pieces[i], pieces[0].shape[0], 0, pd, po, near, far)
    table = {}
    for i in range(2):
        table[2 * i, 2 * i] = lambda i=i: near[i, :width]
        table[2 * i, 2 * i + 1] = lambda i=i: near[i, width : 2 * width]
        table[2 * i + 1, 2 * i + 1] = lambda i=i: near[i, 2 * width : 3 * width]
        for j in range(2):
            table[i, 2 + j] = lambda i=i, j=j: far[(i * 2 + j) * width : (i * 2 + j + 1) * width]
    norm = jnp.zeros((8, LANES), F32)
    for (i, j), read in table.items():
        block = read()
        squares = jnp.sum((block * block).reshape(-1, 8, LANES), axis=0)
        norm = norm + (squares if i == j else 2.0 * squares)
    factor = lax.rsqrt(jnp.sum(norm, keepdims=True) + 1e-06)
    eye = lax.broadcasted_iota(jnp.int32, (width, width), 0) == lax.broadcasted_iota(jnp.int32, (width, width), 1)
    for (i, j), read in table.items():
        block = read()
        for a, b, v in ((i, j, block),) + (() if i == j else ((j, i, block.T),)):
            rows, cols = pl.ds(a * width, width), pl.ds(b * width, width)
            full[rows, cols] = v
            v = v * factor
            put(errors, highs, lows, 0, rows, cols, v)
            put(its, ihighs, ilows, 1, rows, cols, jnp.where(eye, 2.0, 0.0) - v if a == b else -v)
    scale[...] = jnp.broadcast_to(factor, scale.shape)
    steps(0, stop, *tables, None)
    error[...], iterate[...] = errors[stop % 2], its[stop % 2]


def reflect_kernel(width, xd, xo, ours, theirs, inv, out, cross, last, near, far, high, low):
    core = lax.axis_index("core")
    depth = ours.shape[1]
    for gathered, home in ((ours, core), (theirs, 1 - core)):
        gather_blocks(lambda i: gathered.at[i], depth, 0, xd, xo, near, far)
        for i in range(2):
            for j in range(2):
                places = (
                    (at(2 * i + home, width), at(2 * i + j, width), near[i, j * width : (j + 1) * width]),
                    (at(2 * home + i, width), at(2 * (1 - home) + j, width), far[(i * 2 + j) * width : (i * 2 + j + 1) * width]),
                )
                for rows, cols, value in places:
                    cross[rows, cols] = value
                    high[rows, cols], low[rows, cols] = halves(value)
    xy = lax.axis_index("x") * 2 + lax.axis_index("y")
    last[...] = ours[xy ^ 3, lax.rem(lax.axis_index("z") + 1, depth), xd + xo : xd + xo + 8]
    for chosen, product in ((0, dot_first), (1, dot)):

        @pl.when(core == chosen)
        def _():
            value = product(high[...], inv[0]) + product(high[...], inv[1]) + product(low[...], inv[0])
            out[...] = (-value).astype(BF16)


def update_cross_kernel(each, here, shifted, edge, ours, theirs, out, late, *refs):
    packed, (refl, ahead, flat) = refs[:4], refs[4:]
    by_kind(ours, theirs, refl)
    update_edge(edge, refl, ahead)
    update(here, shifted, refl, out)
    delay(out.at[1], ahead, late)
    channels = here.shape[2]
    value = dot_first(out[0, :, at(lax.axis_index("core"), channels // 2)], late[...])
    emit([value[:, j : j + LANES] for j in range(0, channels, LANES)], flat, packed, 0, each)


def there_kernel(width, both, across, both_core, across_core, edge, ours, theirs, out, late, refl, raw, shifted, ahead):
    y, core = lax.axis_index("y"), lax.axis_index("core")
    by_kind(ours, theirs, refl)
    rows = at(1 - y, raw.shape[1])
    raw[:, :, at(y * 2 + core, width)], raw[:, :, at(y * 2 + 1 - core, width)] = both[:, rows], both_core[:, rows]
    raw[:, :, at((1 - y) * 2 + core, width)] = across[...]
    raw[:, :, at((1 - y) * 2 + 1 - core, width)] = across_core[...]
    delay(raw.at[1], edge.at[1], shifted)
    update_edge(edge, refl, ahead)
    update(raw, shifted, refl, out)
    delay(out.at[1], ahead, late)


def predict_kernel(own, other, cross, theirs, last, work, scale, row):
    core = lax.axis_index("core")
    channels = own.shape[0]
    refl = theirs[...]
    for chosen, product in ((0, dot_last), (1, dot)):

        @pl.when(core == chosen)
        def _():
            parts = thirds(cross[...])
            work[...] = product(refl, parts[2]) + product(refl, parts[1]) + product(refl, parts[0])

    mixed = work[...]
    total = own[...] + (mixed + mixed.T)
    parts = thirds(other[...])
    parts = thirds(dot(refl, parts[2]) + dot(refl, parts[1]) + dot(refl, parts[0]))
    work[...] = total + (dot_last(parts[2], refl) + dot_last(parts[1], refl) + dot_last(parts[0], refl))

    @pl.when(core == 1)
    def _():
        row[...] = jnp.zeros_like(row)
        for i in range(2):
            for j in range(4):
                row[i, 0:1, j * LANES : (j + 1) * LANES] = last[i * 4 + j : i * 4 + j + 1]
        end = (row[1] + dot_last(row[0].astype(BF16), refl)).astype(BF16)
        work[...] -= dot_first(end, end)

    total = work[...]
    norm = jnp.sum((total * total).reshape(-1, 8, channels), axis=0)
    factor = lax.rsqrt(jnp.sum(norm, keepdims=True) + 1e-06)
    scale[...] = jnp.broadcast_to(factor, scale.shape)


def begin_kernel(stop, matrix, scale, error, iterate, *tables):
    errors, highs, lows, its, ihighs, ilows = tables
    channels = matrix.shape[0]
    factor = scale[0:1, 0:1]
    every = pl.ds(0, channels)
    step = 128
    for r in range(0, channels, step):
        rows = pl.ds(r, step)
        value = matrix[rows] * factor
        put(errors, highs, lows, 0, rows, every, value)
        shape = (step, channels)
        eye = lax.broadcasted_iota(jnp.int32, shape, 0) + r == lax.broadcasted_iota(jnp.int32, shape, 1)
        put(its, ihighs, ilows, 1, rows, every, jnp.where(eye, 2.0, 0.0) - value)
    steps(0, stop, *tables, None)
    error[...], iterate[...] = errors[stop % 2], its[stop % 2]


def finish_kernel(start, error, iterate, scale, out, *tables):
    errors, highs, lows, its, ihighs, ilows = tables
    channels = error.shape[0]
    every = pl.ds(0, channels)
    put(errors, highs, lows, start % 2, every, every, error[...])
    put(its, ihighs, ilows, start % 2, every, every, iterate[...])
    factor = scale[0:1, 0:1]

    def finish(rows, value):
        out[0, rows], out[1, rows] = halves(value * factor)

    steps(start, NSTEPS, *tables, finish)


def last_kernel(width, ours, theirs, inv, inv_core, here, shifted, there, there_shifted, forward, backward, flat, high, low):
    y, core = lax.axis_index("y"), lax.axis_index("core")
    channels = here.shape[2]
    half, depth, each = channels // 2, ours.shape[1], ours.shape[2]
    for gathered, home in ((ours, core), (theirs, 1 - core)):
        for i, k, zx, ys in sources(depth):
            flat[at(zx * 2 + ys, each)] = gathered[i, k]
        rows = at(home, half)
        for j in range(channels // LANES):
            cols = pl.ds(j * LANES, LANES)
            high[rows, cols], low[rows, cols] = halves(flat[j * half : (j + 1) * half])
    mine = at(y * 2 + core, width)

    def reflect(lefts, rights, product):
        value = product(lefts[0], rights[0]) + product(lefts[0], rights[1]) + product(lefts[1], rights[0])
        return (-value).astype(BF16)

    def final(of_fwd, of_bwd):
        left = reflect((high[mine], low[mine]), (of_bwd[0], of_bwd[1]), dot)
        right = reflect((high[:, mine], low[:, mine]), (of_fwd[0], of_fwd[1]), dot_first)
        for time, both, late in ((y, here, shifted), (1 - y, there, there_shifted)):
            rows = at(time, here.shape[1])
            forward[rows] = (both[0, :, mine].astype(F32) + dot_last(late[...], left)).astype(BF16)
            backward[rows] = (late[:, mine].astype(F32) + dot_last(both[0], right)).astype(BF16)

    @pl.when(core == 0)
    def _():
        final(inv, inv_core)

    @pl.when(core == 1)
    def _():
        final(inv_core, inv)


def ahead(piece, by):
    size = lax.axis_size("z")
    return lax.ppermute(piece, "z", [(i, (i + by) % size) for i in range(size)])


def exchange(pieces):
    both = [(i, 3 - i) for i in range(4)]
    return [pieces[0], swap(pieces[1], "y"), swap(pieces[2], "x"), lax.ppermute(pieces[3], ("x", "y"), both)]


def scatter_z(pieces):
    total = sum(pieces[1:], pieces[0])
    return sum((ahead(total[k], k) for k in range(1, total.shape[0])), total[0])


def z_gather(piece):
    return jnp.stack([piece] + [ahead(piece, by) for by in range(1, lax.axis_size("z"))])


def xy_gather(piece):
    return exchange([piece] * 4)


def share(rows, parts):
    return -(-rows // (8 * parts)) * 8


def local(fwd_in, bwd_in):
    y = lax.axis_index("y")
    zx = ("z", "x")
    samples, width = fwd_in.shape
    half, pair, channels = samples // 2, 2 * width, 4 * width
    depth, near_parts, parts = lax.axis_size("z"), lax.axis_size(zx), lax.axis_size(PARTS)
    pd, xd = share(3 * width, near_parts), share(2 * width, near_parts)
    po, xo = share(4 * width, parts), share(4 * width, parts)
    each = share(8 * width, parts)
    shape = jax.ShapeDtypeStruct
    square = lambda *lead: pltpu.VMEM(lead + (channels, channels), F32)
    square16 = lambda *lead: pltpu.VMEM(lead + (channels, channels), BF16)
    tables = [square(2), square16(2), square16(2)] * 2
    flat = lambda *rows: pltpu.VMEM((max(rows), LANES), F32)
    kernel = functools.partial

    halo = from_behind(jnp.stack([fwd_in[samples - 16 :], bwd_in[samples - 16 :]]), zx)
    cut = lambda which: jnp.stack([lax.dynamic_slice_in_dim(a, which * half, half, 0) for a in (fwd_in, bwd_in)])
    other = cut(1 - y)
    across = swap(other, "y")
    both = jnp.stack([after(fwd_in, other), bwd_in])
    both_core = swap(both, "core")
    halo_core = swap(halo, "core")
    halo_y = swap(jnp.where(y == 0, both[:, half - 16 : half], halo), "y")
    near = call(
        kernel(near_kernel, width, pd, xd),
        [shape((depth, pd + xd, LANES), F32)] * 2,
        [pltpu.VMEM((samples, pair), BF16)] * 3 + [pltpu.VMEM((16, pair), BF16), flat(near_parts * pd, near_parts * xd)],
        3 * samples * pair * pair,
        both, both_core, halo, halo_core,
    )
    near_x = swap(near[1], "x")
    halo_y_core = swap(after(halo_y, near[1]), "core")
    across = after(across, near[1], halo_y_core)
    across2 = swap(after(cut(y), across), "y")
    across_core = swap(across, "core")
    here, edge, shifted, *far, tails = call(
        kernel(far_kernel, width, po, xo),
        [
            shape((2, half, channels), BF16),
            shape((2, 16, channels), BF16),
            shape((half, channels), BF16),
            *[shape((depth, po + xo, LANES), F32)] * 4,
            shape((8, LANES), F32),
        ],
        [pltpu.VMEM((half, channels), BF16), flat(parts * po, parts * xo)],
        4 * half * pair * pair,
        both, across, both_core, across_core, halo, halo_core, halo_y, halo_y_core,
    )
    near_sum = scatter_z([after(near[0], far[0]), near_x])
    swapped = exchange(far)
    far_sum = scatter_z([after(swapped[0], across2)] + swapped[1:])
    chunk = jnp.concatenate([near_sum[:pd], far_sum[:po], near_sum[pd:], far_sum[po:], tails])
    column = z_gather(chunk)
    pieces = xy_gather(column[:, : pd + po])
    stop = NSTEPS // 2
    state = [shape((channels, channels), F32)] * 2 + [shape((8, LANES), F32)]
    full, error, iterate, scale = call(
        kernel(inverse_kernel, width, pd, po, stop),
        [shape((channels, channels), F32)] + state,
        [pltpu.VMEM((2, near_parts * pd, LANES), F32), flat(parts * po)] + tables,
        30 * channels**3,
        *pieces,
    )
    ours = jnp.stack(xy_gather(after(column[:, pd + po :], *pieces)))
    theirs = swap(after(ours, error), "core")
    finish = lambda *args: call(
        kernel(finish_kernel, stop), [shape((2, channels, channels), BF16)], tables, 30 * channels**3, *args
    )[0]
    inv = finish(error, iterate, scale)
    refl, cross, last = call(
        kernel(reflect_kernel, width, xd, xo),
        [shape((channels, channels), BF16), shape((channels, channels), F32), shape((8, LANES), F32)],
        [pltpu.VMEM((2, near_parts * xd, LANES), F32), flat(parts * xo), square16(), square16()],
        6 * channels**3,
        ours, theirs, inv,
    )
    refl_core = swap(refl, "core")
    here2, shifted2, *packed = call(
        kernel(update_cross_kernel, each),
        [shape((2, half, channels), BF16), shape((half, channels), BF16)] + [shape((depth, each, LANES), F32)] * 4,
        [square16(2), pltpu.VMEM((16, channels), BF16), flat(parts * each)],
        5 * half * channels * channels,
        here, shifted, edge, refl, refl_core,
    )
    across2_core = swap(after(across2, column), "core")
    full_core = swap(after(full, refl_core), "core")
    matrix2, scale2 = call(
        predict_kernel,
        [shape((channels, channels), F32), shape((8, LANES), F32)],
        [pltpu.VMEM((2, 16, channels), F32)],
        18 * channels**3,
        after(full, packed[0]), full_core, cross, refl_core, last,
    )
    error2, iterate2 = call(
        kernel(begin_kernel, stop), state[:2], tables, 30 * channels**3, matrix2, scale2
    )
    swapped = exchange(packed)
    cross_sum = after(scatter_z([after(swapped[0], matrix2)] + swapped[1:]), error2)
    inv2 = finish(after(error2, cross_sum), iterate2, scale2)
    inv2_core = swap(inv2, "core")
    column2 = z_gather(cross_sum)
    tail = here[:, half - 16 :]
    edge2 = jnp.where(y == 0, tail, from_behind(tail, zx))
    there2, there_shifted2 = call(
        kernel(there_kernel, width),
        [shape((2, half, channels), BF16), shape((half, channels), BF16)],
        [square16(2), pltpu.VMEM((2, half, channels), BF16), pltpu.VMEM((half, channels), BF16), pltpu.VMEM((16, channels), BF16)],
        4 * half * channels * channels,
        both, across2, both_core, across2_core, edge2, refl, after(refl_core, column2),
    )
    ours2 = jnp.stack(xy_gather(after(column2, inv2)))
    theirs2 = swap(after(ours2, there2), "core")
    return call(
        kernel(last_kernel, width),
        [shape((samples, width), BF16)] * 2,
        [flat(parts * each), square16(), square16()],
        4 * samples * channels * width,
        ours2, theirs2, inv2, inv2_core, here2, shifted2, there2, there_shifted2,
    )


def solution(mesh):
    tm, chan = mesh.shape["tm"], mesh.shape["chan"]
    split = Mesh(mesh.devices.reshape(tm // 2, 2, chan // 2, 2), ("z", "x", "y", "core"))
    spec = P(("z", "x"), ("y", "core"))
    return jax.shard_map(local, mesh=split, in_specs=(spec, spec), out_specs=(spec, spec), check_vma=False)
```

```python
import functools

import jax
import jax.numpy as jnp
from jax import lax
from jax.experimental import pallas as pl
from jax.experimental.pallas import tpu as pltpu
from jax.sharding import Mesh, PartitionSpec as P

ORDERS = 2
NSTEPS = 6
F32 = jnp.float32
BF16 = jnp.bfloat16
PARTS = ("z", "x", "y")
LANES = 128
VMEM = pl.BlockSpec(memory_space=pltpu.VMEM)


def swap(value, axis):
    return lax.ppermute(value, axis, [(0, 1), (1, 0)])


def from_behind(value, axes):
    devices = lax.axis_size(axes)
    return lax.ppermute(value, axes, [(i, i + 1) for i in range(devices - 1)])


def after(value, *others):
    return lax.optimization_barrier((value,) + others)[0]


def call(body, shapes, scratch, flops, *args):
    size = sum(a.size * a.dtype.itemsize for a in args) + sum(s.size * s.dtype.itemsize for s in shapes)
    return pl.pallas_call(
        body,
        out_shape=shapes,
        in_specs=[VMEM] * len(args),
        out_specs=[VMEM] * len(shapes),
        scratch_shapes=scratch,
        compiler_params=pltpu.CompilerParams(vmem_limit_bytes=16 << 20),
        cost_estimate=pl.CostEstimate(flops=flops, bytes_accessed=size, transcendentals=0),
    )(*args)


def dot(a, b):
    return jnp.dot(a, b, preferred_element_type=F32)


def dot_first(a, b):
    return lax.dot_general(a, b, (((0,), (0,)), ((), ())), preferred_element_type=F32)


def dot_last(a, b):
    return lax.dot_general(a, b, (((1,), (1,)), ((), ())), preferred_element_type=F32)


def halves(value):
    high = value.astype(BF16)
    return high, (value - high.astype(F32)).astype(BF16)


def thirds(value):
    high, rest = value.astype(BF16), value - value.astype(BF16).astype(F32)
    return (high,) + halves(rest)


def at(index, size):
    return pl.ds(pl.multiple_of(index * size, size), size)


def delay(source, before, out):
    rows = source.shape[0]
    step = min(rows, 256)
    top = lax.broadcasted_iota(jnp.int32, (step, 1), 0) == 0
    for r in range(0, rows, step):
        edge = (before[...] if r == 0 else source[r - 16 : r]).astype(F32)[15:16]
        moved = pltpu.roll(source[r : r + step].astype(F32), 1, 0)
        out[r : r + step] = jnp.where(top, edge, moved).astype(BF16)


def drop_end(samples, here):
    rows = samples.shape[0]

    @pl.when((lax.axis_index("core") == 1) & here)
    def _():
        tail = samples[rows - 16 :].astype(F32)
        inside = lax.broadcasted_iota(jnp.int32, (16, 1), 0) < 15
        samples[rows - 16 :] = jnp.where(inside, tail, 0.0).astype(BF16)


def emit(blocks, flat, outs, start, each, turned=True):
    used = 0
    for block in blocks:
        flat[used : used + block.shape[0]] = block
        used += block.shape[0]
    depth = outs[0].shape[0]
    parts = depth * len(outs)
    if parts * each > used:
        flat[used : parts * each] = jnp.zeros((parts * each - used, LANES), F32)
    z, x, y = lax.axis_index("z"), lax.axis_index("x"), lax.axis_index("y")
    for i, out in enumerate(outs):
        for k in range(depth):
            part = (lax.rem(z + k, depth) if turned else k) * len(outs) + ((x * 2 + y if len(outs) == 4 else x) ^ i)
            out[k, start : start + each] = flat[at(part, each)]


def sources(depth, turned=True):
    z, x, y = lax.axis_index("z"), lax.axis_index("x"), lax.axis_index("y")
    for i in range(4):
        for k in range(depth):
            xs, ys = x ^ (i >> 1), y ^ (i & 1)
            zx = (lax.rem(z + depth - k, depth) if turned else k) * 2 + xs
            yield i, k, zx, ys


def gather_blocks(piece, depth, start, near_each, far_each, near, far):
    for i, k, zx, ys in sources(depth):
        near[ys, at(zx, near_each)] = piece(i)[k, start : start + near_each]
        far[at(zx * 2 + ys, far_each)] = piece(i)[k, start + near_each : start + near_each + far_each]


def steps(first, last, errors, highs, lows, its, ihighs, ilows, finish):
    channels = errors.shape[1]
    step = channels // 2
    for n in range(first, last):
        now, later = n % 2, (n + 1) % 2
        for r in range(0, channels, step):
            rows = pl.ds(r, step)
            high, low = highs[now, rows], lows[now, rows]
            if n < NSTEPS - 1:
                value = dot(high, highs[now]) + dot(high, lows[now]) + dot(low, highs[now])
                value = 2.0 * errors[now, rows] - value
                errors[later, rows] = value
                highs[later, rows], lows[later, rows] = halves(value)
            if n >= 1:
                value = dot(high, ihighs[now]) + dot(high, ilows[now]) + dot(low, ihighs[now])
                value = 2.0 * its[now, rows] - value
                if n == NSTEPS - 1:
                    finish(rows, value)
                else:
                    its[later, rows] = value
                    ihighs[later, rows], ilows[later, rows] = halves(value)


def put(table, high, low, slot, rows, cols, value):
    table[slot, rows, cols] = value
    high[slot, rows, cols], low[slot, rows, cols] = halves(value)


def by_kind(ours, theirs, refl):
    core = lax.axis_index("core")
    refl[1 - core] = ours[...]
    refl[core] = theirs[...]


def update(both, shifted, refl, out):
    step = 256
    for r in range(0, both.shape[1], step):
        rows = slice(r, r + step)
        forward, backward = both[0, rows], shifted[rows]
        out[0, rows] = (forward.astype(F32) + dot_last(backward, refl[0])).astype(BF16)
        out[1, rows] = (backward.astype(F32) + dot_last(forward, refl[1])).astype(BF16)


def update_edge(edge, refl, out):
    late = pltpu.roll(edge[1].astype(F32), 1, 0)
    out[...] = (late + dot_last(edge[0], refl[1])).astype(BF16)


def near_kernel(width, pd, xd, forward, backward, forward_core, backward_core, halo, halo_core, *refs):
    packed, (chosen, behind, late, edge, flat) = refs[:2], refs[2:]
    core = lax.axis_index("core")
    own, other = at(core, width), at(1 - core, width)
    behind[:, own], behind[:, other] = backward[...], backward_core[...]
    edge[:, own], edge[:, other] = halo[1], halo_core[1]

    @pl.when(core == 0)
    def _():
        chosen[:, own], chosen[:, other] = forward[...], forward_core[...]

    @pl.when(core == 1)
    def _():
        chosen[...] = behind[...]

    zx = ("z", "x")
    drop_end(chosen, lax.axis_index(zx) == lax.axis_size(zx) - 1)
    value = dot_first(chosen[...], chosen[...])
    emit([value[:width, :width], value[:width, width:], value[width:, width:]], flat, packed, 0, pd)
    delay(behind, edge, late)
    value = dot_first(forward[...], late[...])
    emit([value[:, :width], value[:, width:]], flat, packed, pd, xd)


def far_kernel(width, po, xo, *refs):
    own, across, halos = (refs[0:2], refs[2:4]), (refs[4:6], refs[6:8]), refs[8:12]
    (here, edges, shifted), packed, (tails, samples, flat) = refs[12:15], refs[15:19], refs[19:]
    y, core = lax.axis_index("y"), lax.axis_index("core")
    half = here.shape[1]
    pair = 2 * width
    rows = at(y, half)
    for c in range(2):
        mine = at(y * 2 + (core ^ c), width)
        over = at((1 - y) * 2 + (core ^ c), width)
        for kind in range(2):
            here[kind, :, mine] = own[c][kind][rows]
            here[kind, :, over] = across[c][kind][...]
            edges[1, kind, :, mine] = own[c][kind][half - 16 : half]
        edges[0, :, :, mine] = halos[c][...]
        edges[:, :, :, over] = halos[2 + c][...]
    samples[...] = here[core]
    drop_end(samples, lax.axis_index(PARTS) == lax.axis_size(PARTS) - 1)
    value = dot_first(samples[:, :pair], samples[:, pair:])
    blocks = lambda v: [v[i : i + width, j : j + width] for i in (0, width) for j in (0, width)]
    emit(blocks(value), flat, packed, 0, po)
    delay(here.at[1], edges.at[y, 1], shifted)
    value = dot_first(here[0, :, at(core, pair)], shifted[:, at(1 - core, pair)])
    emit(blocks(value), flat, packed, po, xo)
    for i, rows in enumerate((here[0, half - 16 :], shifted[half - 16 :])):
        row = rows.astype(F32)[15:16]
        for j in range(4):
            tails[i * 4 + j : i * 4 + j + 1] = row[:, j * LANES : (j + 1) * LANES]


def inverse_kernel(width, pd, po, stop, *refs):
    pieces, (full, error, iterate, scale), (near, far) = refs[:4], refs[4:8], refs[8:10]
    tables = refs[10:]
    errors, highs, lows, its, ihighs, ilows = tables
    gather_blocks(lambda i: pieces[i], pieces[0].shape[0], 0, pd, po, near, far)
    table = {}
    for i in range(2):
        table[2 * i, 2 * i] = lambda i=i: near[i, :width]
        table[2 * i, 2 * i + 1] = lambda i=i: near[i, width : 2 * width]
        table[2 * i + 1, 2 * i + 1] = lambda i=i: near[i, 2 * width : 3 * width]
        for j in range(2):
            table[i, 2 + j] = lambda i=i, j=j: far[(i * 2 + j) * width : (i * 2 + j + 1) * width]
    norm = jnp.zeros((8, LANES), F32)
    for (i, j), read in table.items():
        block = read()
        squares = jnp.sum((block * block).reshape(-1, 8, LANES), axis=0)
        norm = norm + (squares if i == j else 2.0 * squares)
    factor = lax.rsqrt(jnp.sum(norm, keepdims=True) + 1e-06)
    eye = lax.broadcasted_iota(jnp.int32, (width, width), 0) == lax.broadcasted_iota(jnp.int32, (width, width), 1)
    for (i, j), read in table.items():
        block = read()
        for a, b, v in ((i, j, block),) + (() if i == j else ((j, i, block.T),)):
            rows, cols = pl.ds(a * width, width), pl.ds(b * width, width)
            full[rows, cols] = v
            v = v * factor
            put(errors, highs, lows, 0, rows, cols, v)
            put(its, ihighs, ilows, 1, rows, cols, jnp.where(eye, 2.0, 0.0) - v if a == b else -v)
    scale[...] = jnp.broadcast_to(factor, scale.shape)
    steps(0, stop, *tables, None)
    error[...], iterate[...] = errors[stop % 2], its[stop % 2]


def reflect_kernel(width, xd, xo, ours, theirs, inv, out, cross, last, near, far, high, low):
    core = lax.axis_index("core")
    depth = ours.shape[1]
    for gathered, home in ((ours, core), (theirs, 1 - core)):
        gather_blocks(lambda i: gathered.at[i], depth, 0, xd, xo, near, far)
        for i in range(2):
            for j in range(2):
                places = (
                    (at(2 * i + home, width), at(2 * i + j, width), near[i, j * width : (j + 1) * width]),
                    (at(2 * home + i, width), at(2 * (1 - home) + j, width), far[(i * 2 + j) * width : (i * 2 + j + 1) * width]),
                )
                for rows, cols, value in places:
                    cross[rows, cols] = value
                    high[rows, cols], low[rows, cols] = halves(value)
    xy = lax.axis_index("x") * 2 + lax.axis_index("y")
    last[...] = ours[xy ^ 3, lax.rem(lax.axis_index("z") + 1, depth), xd + xo : xd + xo + 8]
    for chosen, product in ((0, dot_first), (1, dot)):

        @pl.when(core == chosen)
        def _():
            value = product(high[...], inv[0]) + product(high[...], inv[1]) + product(low[...], inv[0])
            out[...] = (-value).astype(BF16)


def update_cross_kernel(each, here, shifted, edges, ours, theirs, out, late, *refs):
    packed, (refl, ahead, flat) = refs[:4], refs[4:]
    by_kind(ours, theirs, refl)
    update_edge(edges.at[lax.axis_index("y")], refl, ahead)
    update(here, shifted, refl, out)
    delay(out.at[1], ahead, late)
    channels = here.shape[2]
    value = dot_first(out[0, :, at(lax.axis_index("core"), channels // 2)], late[...])
    emit([value[:, j : j + LANES] for j in range(0, channels, LANES)], flat, packed, 0, each, turned=False)


def there_kernel(width, *refs):
    own, across, (edges, ours, theirs) = (refs[0:2], refs[2:4]), (refs[4:6], refs[6:8]), refs[8:11]
    out, late, refl, raw, shifted, ahead = refs[11:]
    y, core = lax.axis_index("y"), lax.axis_index("core")
    by_kind(ours, theirs, refl)
    edge = edges.at[1 - y]
    rows = at(1 - y, raw.shape[1])
    for c in range(2):
        for kind in range(2):
            raw[kind, :, at(y * 2 + (core ^ c), width)] = own[c][kind][rows]
            raw[kind, :, at((1 - y) * 2 + (core ^ c), width)] = across[c][kind][...]
    delay(raw.at[1], edge.at[1], shifted)
    update_edge(edge, refl, ahead)
    update(raw, shifted, refl, out)
    delay(out.at[1], ahead, late)


def predict_kernel(own, other, cross, theirs, last, work, scale, row):
    core = lax.axis_index("core")
    channels = own.shape[0]
    refl = theirs[...]
    for chosen, product in ((0, dot_last), (1, dot)):

        @pl.when(core == chosen)
        def _():
            parts = thirds(cross[...])
            work[...] = product(refl, parts[2]) + product(refl, parts[1]) + product(refl, parts[0])

    mixed = work[...]
    total = own[...] + (mixed + mixed.T)
    parts = thirds(other[...])
    parts = thirds(dot(refl, parts[2]) + dot(refl, parts[1]) + dot(refl, parts[0]))
    work[...] = total + (dot_last(parts[2], refl) + dot_last(parts[1], refl) + dot_last(parts[0], refl))

    @pl.when(core == 1)
    def _():
        row[...] = jnp.zeros_like(row)
        for i in range(2):
            for j in range(4):
                row[i, 0:1, j * LANES : (j + 1) * LANES] = last[i * 4 + j : i * 4 + j + 1]
        end = (row[1] + dot_last(row[0].astype(BF16), refl)).astype(BF16)
        work[...] -= dot_first(end, end)

    total = work[...]
    norm = jnp.sum((total * total).reshape(-1, 8, channels), axis=0)
    factor = lax.rsqrt(jnp.sum(norm, keepdims=True) + 1e-06)
    scale[...] = jnp.broadcast_to(factor, scale.shape)


def begin_kernel(stop, matrix, scale, error, iterate, *tables):
    errors, highs, lows, its, ihighs, ilows = tables
    channels = matrix.shape[0]
    factor = scale[0:1, 0:1]
    every = pl.ds(0, channels)
    step = 128
    for r in range(0, channels, step):
        rows = pl.ds(r, step)
        value = matrix[rows] * factor
        put(errors, highs, lows, 0, rows, every, value)
        shape = (step, channels)
        eye = lax.broadcasted_iota(jnp.int32, shape, 0) + r == lax.broadcasted_iota(jnp.int32, shape, 1)
        put(its, ihighs, ilows, 1, rows, every, jnp.where(eye, 2.0, 0.0) - value)
    steps(0, stop, *tables, None)
    error[...], iterate[...] = errors[stop % 2], its[stop % 2]


def finish_kernel(start, error, iterate, scale, out, *tables):
    errors, highs, lows, its, ihighs, ilows = tables
    channels = error.shape[0]
    every = pl.ds(0, channels)
    put(errors, highs, lows, start % 2, every, every, error[...])
    put(its, ihighs, ilows, start % 2, every, every, iterate[...])
    factor = scale[0:1, 0:1]

    def finish(rows, value):
        out[0, rows], out[1, rows] = halves(value * factor)

    steps(start, NSTEPS, *tables, finish)


def last_kernel(width, ours, theirs, inv, inv_core, here, shifted, there, there_shifted, forward, backward, flat, high, low):
    y, core = lax.axis_index("y"), lax.axis_index("core")
    channels = here.shape[2]
    half, depth, each = channels // 2, ours.shape[1], ours.shape[2]
    for gathered, home in ((ours, core), (theirs, 1 - core)):
        for i, k, zx, ys in sources(depth, turned=False):
            flat[at(zx * 2 + ys, each)] = gathered[i, k]
        rows = at(home, half)
        for j in range(channels // LANES):
            cols = pl.ds(j * LANES, LANES)
            high[rows, cols], low[rows, cols] = halves(flat[j * half : (j + 1) * half])
    mine = at(y * 2 + core, width)

    def reflect(lefts, rights, product):
        value = product(lefts[0], rights[0]) + product(lefts[0], rights[1]) + product(lefts[1], rights[0])
        return (-value).astype(BF16)

    def final(of_fwd, of_bwd):
        left = reflect((high[mine], low[mine]), (of_bwd[0], of_bwd[1]), dot)
        right = reflect((high[:, mine], low[:, mine]), (of_fwd[0], of_fwd[1]), dot_first)
        for time, both, late in ((y, here, shifted), (1 - y, there, there_shifted)):
            rows = at(time, here.shape[1])
            forward[rows] = (both[0, :, mine].astype(F32) + dot_last(late[...], left)).astype(BF16)
            backward[rows] = (late[:, mine].astype(F32) + dot_last(both[0], right)).astype(BF16)

    @pl.when(core == 0)
    def _():
        final(inv, inv_core)

    @pl.when(core == 1)
    def _():
        final(inv_core, inv)


def ahead(piece, by):
    size = lax.axis_size("z")
    return lax.ppermute(piece, "z", [(i, (i + by) % size) for i in range(size)])


def exchange(pieces):
    both = [(i, 3 - i) for i in range(4)]
    return [pieces[0], swap(pieces[1], "y"), swap(pieces[2], "x"), lax.ppermute(pieces[3], ("x", "y"), both)]


def scatter_z(pieces):
    total = sum(pieces[1:], pieces[0])
    return sum((ahead(total[k], k) for k in range(1, total.shape[0])), total[0])


def z_gather(piece):
    return jnp.stack([piece] + [ahead(piece, by) for by in range(1, lax.axis_size("z"))])


def xy_gather(piece):
    return exchange([piece] * 4)


def share(rows, parts):
    return -(-rows // (8 * parts)) * 8


def local(fwd_in, bwd_in):
    y = lax.axis_index("y")
    zx = ("z", "x")
    samples, width = fwd_in.shape
    half, pair, channels = samples // 2, 2 * width, 4 * width
    depth, near_parts, parts = lax.axis_size("z"), lax.axis_size(zx), lax.axis_size(PARTS)
    pd, xd = share(3 * width, near_parts), share(2 * width, near_parts)
    po, xo = share(4 * width, parts), share(4 * width, parts)
    each = share(8 * width, parts)
    shape = jax.ShapeDtypeStruct
    square = lambda *lead: pltpu.VMEM(lead + (channels, channels), F32)
    square16 = lambda *lead: pltpu.VMEM(lead + (channels, channels), BF16)
    tables = [square(2), square16(2), square16(2)] * 2
    flat = lambda *rows: pltpu.VMEM((max(rows), LANES), F32)
    kernel = functools.partial

    own = (fwd_in, bwd_in)
    cut = lambda which: [lax.dynamic_slice_in_dim(a, which * half, half, 0) for a in own]
    across = [swap(a, "y") for a in cut(1 - y)]
    tail = lambda end: jnp.stack([a[end - 16 : end] for a in own])
    halo = from_behind(tail(samples), zx)
    own_core = [swap(a, "core") for a in own]
    halo_core = swap(halo, "core")
    halo_y = swap(jnp.stack([halo, tail(half)]), "y")
    near = call(
        kernel(near_kernel, width, pd, xd),
        [shape((depth, pd + xd, LANES), F32)] * 2,
        [pltpu.VMEM((samples, pair), BF16)] * 3 + [pltpu.VMEM((16, pair), BF16), flat(near_parts * pd, near_parts * xd)],
        3 * samples * pair * pair,
        *own, *own_core, halo, halo_core,
    )
    near_x = swap(near[1], "x")
    halo_y_core = swap(after(halo_y, near[1]), "core")
    across_core = [swap(across[0], "core"), swap(after(across[1], near[1]), "core")]
    here, edges, shifted, *far, tails = call(
        kernel(far_kernel, width, po, xo),
        [
            shape((2, half, channels), BF16),
            shape((2, 2, 16, channels), BF16),
            shape((half, channels), BF16),
            *[shape((depth, po + xo, LANES), F32)] * 4,
            shape((8, LANES), F32),
        ],
        [pltpu.VMEM((half, channels), BF16), flat(parts * po, parts * xo)],
        4 * half * pair * pair,
        *own, *own_core, *across, *across_core, halo, halo_core, halo_y, halo_y_core,
    )
    near_sum = scatter_z([after(near[0], far[0]), near_x])
    swapped = exchange(far)
    swapped[0] = after(swapped[0], near_sum)
    across2 = [swap(after(a, swapped[1]), "y") for a in cut(y)]
    far_sum = scatter_z(swapped)
    chunk = jnp.concatenate([near_sum[:pd], far_sum[:po], near_sum[pd:], far_sum[po:], tails])
    column = z_gather(chunk)
    pieces = xy_gather(after(column[:, : pd + po], *across2))
    stop = NSTEPS // 2
    state = [shape((channels, channels), F32)] * 2 + [shape((8, LANES), F32)]
    full, error, iterate, scale = call(
        kernel(inverse_kernel, width, pd, po, stop),
        [shape((channels, channels), F32)] + state,
        [pltpu.VMEM((2, near_parts * pd, LANES), F32), flat(parts * po)] + tables,
        30 * channels**3,
        *pieces,
    )
    ours = jnp.stack(xy_gather(after(column[:, pd + po :], *pieces)))
    theirs = swap(after(ours, error), "core")
    finish = lambda *args: call(
        kernel(finish_kernel, stop), [shape((2, channels, channels), BF16)], tables, 30 * channels**3, *args
    )[0]
    inv = finish(error, iterate, scale)
    refl, cross, last = call(
        kernel(reflect_kernel, width, xd, xo),
        [shape((channels, channels), BF16), shape((channels, channels), F32), shape((8, LANES), F32)],
        [pltpu.VMEM((2, near_parts * xd, LANES), F32), flat(parts * xo), square16(), square16()],
        6 * channels**3,
        ours, theirs, inv,
    )
    refl_core = swap(refl, "core")
    here2, shifted2, *packed = call(
        kernel(update_cross_kernel, each),
        [shape((2, half, channels), BF16), shape((half, channels), BF16)] + [shape((depth, each, LANES), F32)] * 4,
        [square16(2), pltpu.VMEM((16, channels), BF16), flat(parts * each)],
        5 * half * channels * channels,
        here, shifted, edges, refl, refl_core,
    )
    across2_core = [swap(a, "core") for a in across2]
    full_core = swap(after(full, refl_core), "core")
    matrix2, scale2 = call(
        predict_kernel,
        [shape((channels, channels), F32), shape((8, LANES), F32)],
        [pltpu.VMEM((2, 16, channels), F32)],
        18 * channels**3,
        after(full, packed[0]), full_core, cross, refl_core, last,
    )
    error2, iterate2 = call(
        kernel(begin_kernel, stop), state[:2], tables, 30 * channels**3, matrix2, scale2
    )
    swapped = exchange(packed)
    swapped[0] = after(swapped[0], matrix2)
    column2 = jnp.sum(z_gather(sum(swapped[1:], swapped[0])), axis=0)
    inv2 = finish(error2, iterate2, scale2)
    inv2_core = swap(inv2, "core")
    there2, there_shifted2 = call(
        kernel(there_kernel, width),
        [shape((2, half, channels), BF16), shape((half, channels), BF16)],
        [square16(2), pltpu.VMEM((2, half, channels), BF16), pltpu.VMEM((half, channels), BF16), pltpu.VMEM((16, channels), BF16)],
        4 * half * channels * channels,
        *own, *own_core, *across2, *across2_core, edges, refl, after(refl_core, column2),
    )
    ours2 = jnp.stack(xy_gather(after(column2, inv2)))
    theirs2 = swap(after(ours2, there2), "core")
    return call(
        kernel(last_kernel, width),
        [shape((samples, width), BF16)] * 2,
        [flat(parts * each), square16(), square16()],
        4 * samples * channels * width,
        ours2, theirs2, inv2, inv2_core, here2, shifted2, there2, there_shifted2,
    )


def solution(mesh):
    tm, chan = mesh.shape["tm"], mesh.shape["chan"]
    split = Mesh(mesh.devices.reshape(tm // 2, 2, chan // 2, 2), ("z", "x", "y", "core"))
    spec = P(("z", "x"), ("y", "core"))
    return jax.shard_map(local, mesh=split, in_specs=(spec, spec), out_specs=(spec, spec), check_vma=False)
```

```python
import functools

import jax
import jax.numpy as jnp
from jax import lax
from jax.experimental import pallas as pl
from jax.experimental.pallas import tpu as pltpu
from jax.sharding import Mesh, PartitionSpec as P

ORDERS = 2
NSTEPS = 6
F32 = jnp.float32
BF16 = jnp.bfloat16
PARTS = ("z", "x", "y")
LANES = 128
VMEM = pl.BlockSpec(memory_space=pltpu.VMEM)


def swap(value, axis):
    return lax.ppermute(value, axis, [(0, 1), (1, 0)])


def from_behind(value, axes):
    devices = lax.axis_size(axes)
    return lax.ppermute(value, axes, [(i, i + 1) for i in range(devices - 1)])


def after(value, *others):
    return lax.optimization_barrier((value,) + others)[0]


def call(body, shapes, scratch, flops, *args, outside=0):
    size = sum(a.size * a.dtype.itemsize for a in args) + sum(s.size * s.dtype.itemsize for s in shapes)
    return pl.pallas_call(
        body,
        out_shape=shapes,
        in_specs=[pl.BlockSpec(memory_space=pltpu.HBM)] * outside + [VMEM] * (len(args) - outside),
        out_specs=[VMEM] * len(shapes),
        scratch_shapes=scratch,
        compiler_params=pltpu.CompilerParams(vmem_limit_bytes=16 << 20),
        cost_estimate=pl.CostEstimate(flops=flops, bytes_accessed=size, transcendentals=0),
    )(*args)


def dot(a, b):
    return jnp.dot(a, b, preferred_element_type=F32)


def dot_first(a, b):
    return lax.dot_general(a, b, (((0,), (0,)), ((), ())), preferred_element_type=F32)


def dot_last(a, b):
    return lax.dot_general(a, b, (((1,), (1,)), ((), ())), preferred_element_type=F32)


def halves(value):
    high = value.astype(BF16)
    return high, (value - high.astype(F32)).astype(BF16)


def thirds(value):
    high, rest = value.astype(BF16), value - value.astype(BF16).astype(F32)
    return (high,) + halves(rest)


def at(index, size):
    return pl.ds(pl.multiple_of(index * size, size), size)


def delay(source, before, out):
    rows = source.shape[0]
    step = min(rows, 256)
    top = lax.broadcasted_iota(jnp.int32, (step, 1), 0) == 0
    for r in range(0, rows, step):
        edge = (before[...] if r == 0 else source[r - 16 : r]).astype(F32)[15:16]
        moved = pltpu.roll(source[r : r + step].astype(F32), 1, 0)
        out[r : r + step] = jnp.where(top, edge, moved).astype(BF16)


def drop_end(samples, here):
    rows = samples.shape[0]

    @pl.when((lax.axis_index("core") == 1) & here)
    def _():
        tail = samples[rows - 16 :].astype(F32)
        inside = lax.broadcasted_iota(jnp.int32, (16, 1), 0) < 15
        samples[rows - 16 :] = jnp.where(inside, tail, 0.0).astype(BF16)


def emit(blocks, flat, outs, start, each, turned=True):
    used = 0
    for block in blocks:
        flat[used : used + block.shape[0]] = block
        used += block.shape[0]
    depth = outs[0].shape[0]
    parts = depth * len(outs)
    if parts * each > used:
        flat[used : parts * each] = jnp.zeros((parts * each - used, LANES), F32)
    z, x, y = lax.axis_index("z"), lax.axis_index("x"), lax.axis_index("y")
    for i, out in enumerate(outs):
        for k in range(depth):
            part = (lax.rem(z + k, depth) if turned else k) * len(outs) + ((x * 2 + y if len(outs) == 4 else x) ^ i)
            out[k, start : start + each] = flat[at(part, each)].astype(out.dtype)


def sources(depth, turned=True):
    z, x, y = lax.axis_index("z"), lax.axis_index("x"), lax.axis_index("y")
    for i in range(4):
        for k in range(depth):
            xs, ys = x ^ (i >> 1), y ^ (i & 1)
            zx = (lax.rem(z + depth - k, depth) if turned else k) * 2 + xs
            yield i, k, zx, ys


def gather_blocks(piece, depth, start, near_each, far_each, near, far):
    for i, k, zx, ys in sources(depth):
        near[ys, at(zx, near_each)] = piece(i)[k, start : start + near_each]
        far[at(zx * 2 + ys, far_each)] = piece(i)[k, start + near_each : start + near_each + far_each]


def steps(first, last, errors, highs, lows, its, ihighs, ilows, finish):
    channels = errors.shape[1]
    half = channels // 2
    top, left, right = slice(0, half), slice(0, half), slice(half, channels)
    for n in range(first, last):
        now, later = n % 2, (n + 1) % 2

        def store(table, high, low, rows, cols, value):
            if n == NSTEPS - 1:
                finish(rows, cols, value)
            else:
                table[later, rows, cols] = value
                high[later, rows, cols], low[later, rows, cols] = halves(value)

        def advance(table, high, low):
            for rows, cols in ((top, slice(0, channels)), (right, right)):
                ahigh, alow = highs[now, rows], lows[now, rows]
                bhigh, blow = high[now, :, cols], low[now, :, cols]
                value = 2.0 * table[now, rows, cols] - (dot(ahigh, bhigh) + dot(ahigh, blow) + dot(alow, bhigh))
                store(table, high, low, rows, cols, value)
                if rows == top:
                    store(table, high, low, right, left, value[:, half:].T)

        if n < NSTEPS - 1:
            advance(errors, highs, lows)
        if n >= 1:
            advance(its, ihighs, ilows)


def put(table, high, low, slot, rows, cols, value):
    table[slot, rows, cols] = value
    high[slot, rows, cols], low[slot, rows, cols] = halves(value)


def by_kind(ours, theirs, refl):
    core = lax.axis_index("core")
    refl[1 - core] = ours[...]
    refl[core] = theirs[...]


def update(both, shifted, refl, out):
    step = 256
    for r in range(0, both.shape[1], step):
        rows = slice(r, r + step)
        forward, backward = both[0, rows], shifted[rows]
        out[0, rows] = (forward.astype(F32) + dot_last(backward, refl[0])).astype(BF16)
        out[1, rows] = (backward.astype(F32) + dot_last(forward, refl[1])).astype(BF16)


def update_edge(edge, refl, out):
    late = pltpu.roll(edge[1].astype(F32), 1, 0)
    out[...] = (late + dot_last(edge[0], refl[1])).astype(BF16)


def copy_all(pairs, sems):
    copies = [pltpu.make_async_copy(source, target, sems.at[i]) for i, (source, target) in enumerate(pairs)]
    for copy in copies:
        copy.start()
    for copy in copies:
        copy.wait()


def cut_kernel(forward, backward, send, tail, sems):
    half, end = send.shape[0], forward.shape[0]
    last = pl.ds(end - 16, 16)
    pairs = [(forward.at[at(1 - lax.axis_index("y"), half)], send)]
    copy_all(pairs + [(forward.at[last], tail.at[0]), (backward.at[last], tail.at[1])], sems)


def front_kernel(forward, backward, halo, send, sems):
    half = forward.shape[0] // 2
    ahead = pl.ds(half - 16, 16)
    pairs = [
        (backward.at[at(1 - lax.axis_index("y"), half)], send.at[pl.ds(64, half)]),
        (forward.at[ahead], send.at[pl.ds(32, 16)]),
        (backward.at[ahead], send.at[pl.ds(48, 16)]),
    ]
    send[0:16], send[16:32] = halo[0], halo[1]
    copy_all(pairs, sems)


def near_kernel(width, pd, xd, forward, backward, forward_core, backward_core, halo, halo_core, *refs):
    packed, back = refs[:2], refs[2]
    chosen, behind, late, edge, flat = refs[3:]
    core = lax.axis_index("core")
    own, other = at(core, width), at(1 - core, width)
    rows = at(lax.axis_index("y"), back.shape[1])
    back[0], back[1] = forward[rows], backward[rows]
    behind[:, own], behind[:, other] = backward[...], backward_core[...]
    edge[:, own], edge[:, other] = halo[1], halo_core[1]

    @pl.when(core == 0)
    def _():
        chosen[:, own], chosen[:, other] = forward[...], forward_core[...]

    @pl.when(core == 1)
    def _():
        chosen[...] = behind[...]

    zx = ("z", "x")
    drop_end(chosen, lax.axis_index(zx) == lax.axis_size(zx) - 1)
    value = dot_first(chosen[...], chosen[...])
    emit([value[:width, :width], value[:width, width:], value[width:, width:]], flat, packed, 0, pd)
    delay(behind, edge, late)
    value = dot_first(forward[...], late[...])
    emit([value[:, :width], value[:, width:]], flat, packed, pd, xd)


def far_kernel(width, po, xo, *refs):
    own, across, halos = (refs[0:2], refs[2:4]), (refs[4:6], refs[6:8]), refs[8:10]
    (here, edges, shifted), packed, (tails, samples, flat) = refs[10:13], refs[13:17], refs[17:]
    y, core = lax.axis_index("y"), lax.axis_index("core")
    half = here.shape[1]
    pair = 2 * width
    rows = at(y, half)
    for c in range(2):
        mine = at(y * 2 + (core ^ c), width)
        over = at((1 - y) * 2 + (core ^ c), width)
        for kind in range(2):
            here[kind, :, mine] = own[c][kind][rows]
            here[kind, :, over] = across[c][kind][64 * kind :]
            edges[0, kind, :, mine] = halos[c][kind]
            edges[1, kind, :, mine] = own[c][kind][half - 16 : half]
            for e in range(2):
                edges[e, kind, :, over] = across[c][1][e * 32 + kind * 16 : e * 32 + kind * 16 + 16]
    samples[...] = here[core]
    drop_end(samples, lax.axis_index(PARTS) == lax.axis_size(PARTS) - 1)
    value = dot_first(samples[:, :pair], samples[:, pair:])
    blocks = lambda v: [v[i : i + width, j : j + width] for i in (0, width) for j in (0, width)]
    emit(blocks(value), flat, packed, 0, po)
    delay(here.at[1], edges.at[y, 1], shifted)
    value = dot_first(here[0, :, at(core, pair)], shifted[:, at(1 - core, pair)])
    emit(blocks(value), flat, packed, po, xo)
    for i, rows in enumerate((here[0, half - 16 :], shifted[half - 16 :])):
        row = rows.astype(F32)[15:16]
        for j in range(4):
            tails[i * 4 + j : i * 4 + j + 1] = row[:, j * LANES : (j + 1) * LANES]


def inverse_kernel(width, pd, po, stop, *refs):
    pieces, (full, error, iterate, scale), (near, far) = refs[:4], refs[4:8], refs[8:10]
    tables = refs[10:]
    errors, highs, lows, its, ihighs, ilows = tables
    gather_blocks(lambda i: pieces[i], pieces[0].shape[0], 0, pd, po, near, far)
    table = {}
    for i in range(2):
        table[2 * i, 2 * i] = lambda i=i: near[i, :width]
        table[2 * i, 2 * i + 1] = lambda i=i: near[i, width : 2 * width]
        table[2 * i + 1, 2 * i + 1] = lambda i=i: near[i, 2 * width : 3 * width]
        for j in range(2):
            table[i, 2 + j] = lambda i=i, j=j: far[(i * 2 + j) * width : (i * 2 + j + 1) * width]
    norm = jnp.zeros((8, LANES), F32)
    for (i, j), read in table.items():
        block = read()
        squares = jnp.sum((block * block).reshape(-1, 8, LANES), axis=0)
        norm = norm + (squares if i == j else 2.0 * squares)
    factor = lax.rsqrt(jnp.sum(norm, keepdims=True) + 1e-06)
    eye = lax.broadcasted_iota(jnp.int32, (width, width), 0) == lax.broadcasted_iota(jnp.int32, (width, width), 1)
    for (i, j), read in table.items():
        block = read()
        for a, b, v in ((i, j, block),) + (() if i == j else ((j, i, block.T),)):
            rows, cols = pl.ds(a * width, width), pl.ds(b * width, width)
            full[rows, cols] = v
            v = v * factor
            put(errors, highs, lows, 0, rows, cols, v)
            put(its, ihighs, ilows, 1, rows, cols, jnp.where(eye, 2.0, 0.0) - v if a == b else -v)
    scale[...] = jnp.broadcast_to(factor, scale.shape)
    steps(0, stop, *tables, None)
    error[...], iterate[...] = errors[stop % 2], its[stop % 2]


def reflect_kernel(width, xd, xo, ours, theirs, inv, out, cross, last, near, far, high, low):
    core = lax.axis_index("core")
    depth = ours.shape[1]
    for gathered, home in ((ours, core), (theirs, 1 - core)):
        gather_blocks(lambda i: gathered.at[i], depth, 0, xd, xo, near, far)
        for i in range(2):
            for j in range(2):
                places = (
                    (at(2 * i + home, width), at(2 * i + j, width), near[i, j * width : (j + 1) * width]),
                    (at(2 * home + i, width), at(2 * (1 - home) + j, width), far[(i * 2 + j) * width : (i * 2 + j + 1) * width]),
                )
                for rows, cols, value in places:
                    cross[rows, cols] = value
                    high[rows, cols], low[rows, cols] = halves(value)
    xy = lax.axis_index("x") * 2 + lax.axis_index("y")
    last[...] = ours[xy ^ 3, lax.rem(lax.axis_index("z") + 1, depth), xd + xo : xd + xo + 8]
    for chosen, product in ((0, dot_first), (1, dot)):

        @pl.when(core == chosen)
        def _():
            value = product(high[...], inv[0]) + product(high[...], inv[1]) + product(low[...], inv[0])
            out[...] = (-value).astype(BF16)


def update_cross_kernel(each, here, shifted, edges, ours, theirs, out, late, *refs):
    packed, (refl, ahead, flat) = refs[:4], refs[4:]
    by_kind(ours, theirs, refl)
    update_edge(edges.at[lax.axis_index("y")], refl, ahead)
    update(here, shifted, refl, out)
    delay(out.at[1], ahead, late)
    channels = here.shape[2]
    value = dot_first(out[0, :, at(lax.axis_index("core"), channels // 2)], late[...])
    emit([value[:, j : j + LANES] for j in range(0, channels, LANES)], flat, packed, 0, each, turned=False)


def there_kernel(width, *refs):
    own, across, (edges, ours, theirs) = (refs[0:2], refs[2:4]), refs[4:6], refs[6:9]
    out, late, refl, raw, shifted, ahead = refs[9:]
    y, core = lax.axis_index("y"), lax.axis_index("core")
    by_kind(ours, theirs, refl)
    edge = edges.at[1 - y]
    rows = at(1 - y, raw.shape[1])
    for c in range(2):
        for kind in range(2):
            raw[kind, :, at(y * 2 + (core ^ c), width)] = own[c][kind][rows]
            raw[kind, :, at((1 - y) * 2 + (core ^ c), width)] = across[c][kind]
    delay(raw.at[1], edge.at[1], shifted)
    update_edge(edge, refl, ahead)
    update(raw, shifted, refl, out)
    delay(out.at[1], ahead, late)


def predict_kernel(own, other, cross, theirs, last, work, scale, row):
    core = lax.axis_index("core")
    channels = own.shape[0]
    refl = theirs[...]
    for chosen, product in ((0, dot_last), (1, dot)):

        @pl.when(core == chosen)
        def _():
            parts = thirds(cross[...])
            work[...] = product(refl, parts[2]) + product(refl, parts[1]) + product(refl, parts[0])

    mixed = work[...]
    total = own[...] + (mixed + mixed.T)
    parts = thirds(other[...])
    parts = thirds(dot(refl, parts[2]) + dot(refl, parts[1]) + dot(refl, parts[0]))
    work[...] = total + (dot_last(parts[2], refl) + dot_last(parts[1], refl) + dot_last(parts[0], refl))

    @pl.when(core == 1)
    def _():
        row[...] = jnp.zeros_like(row)
        for i in range(2):
            for j in range(4):
                row[i, 0:1, j * LANES : (j + 1) * LANES] = last[i * 4 + j : i * 4 + j + 1]
        end = (row[1] + dot_last(row[0].astype(BF16), refl)).astype(BF16)
        work[...] -= dot_first(end, end)

    total = work[...]
    norm = jnp.sum((total * total).reshape(-1, 8, channels), axis=0)
    factor = lax.rsqrt(jnp.sum(norm, keepdims=True) + 1e-06)
    scale[...] = jnp.broadcast_to(factor, scale.shape)


def begin_kernel(stop, matrix, scale, error, iterate, *tables):
    errors, highs, lows, its, ihighs, ilows = tables
    channels = matrix.shape[0]
    factor = scale[0:1, 0:1]
    every = pl.ds(0, channels)
    step = 128
    for r in range(0, channels, step):
        rows = pl.ds(r, step)
        value = matrix[rows] * factor
        put(errors, highs, lows, 0, rows, every, value)
        shape = (step, channels)
        eye = lax.broadcasted_iota(jnp.int32, shape, 0) + r == lax.broadcasted_iota(jnp.int32, shape, 1)
        put(its, ihighs, ilows, 1, rows, every, jnp.where(eye, 2.0, 0.0) - value)
    steps(0, stop, *tables, None)
    error[...], iterate[...] = errors[stop % 2], its[stop % 2]


def finish_kernel(start, error, iterate, scale, out, *tables):
    errors, highs, lows, its, ihighs, ilows = tables
    channels = error.shape[0]
    every = pl.ds(0, channels)
    put(errors, highs, lows, start % 2, every, every, error[...])
    put(its, ihighs, ilows, start % 2, every, every, iterate[...])
    factor = scale[0:1, 0:1]

    def finish(rows, cols, value):
        out[0, rows, cols], out[1, rows, cols] = halves(value * factor)

    steps(start, NSTEPS, *tables, finish)


def last_kernel(width, ours, theirs, inv, inv_core, here, shifted, there, there_shifted, forward, backward, flat, rows_of, cols_of):
    y, core = lax.axis_index("y"), lax.axis_index("core")
    channels = here.shape[2]
    half, depth, each = channels // 2, ours.shape[1], ours.shape[2]
    for gathered, home in ((ours, core), (theirs, 1 - core)):
        for i, k, zx, ys in sources(depth, turned=False):
            flat[home, at(zx * 2 + ys, each)] = gathered[i, k]
    for n in range(channels // LANES):
        value = flat[y, at(2 * n + core, width)]
        rows_of[0, :, n * LANES : (n + 1) * LANES], rows_of[1, :, n * LANES : (n + 1) * LANES] = halves(value)
    for home in range(2):
        value = flat[home, at(y * 2 + core, half)]
        cols_of[0, home * half : (home + 1) * half], cols_of[1, home * half : (home + 1) * half] = halves(value)
    mine = at(y * 2 + core, width)

    def reflect(lefts, rights, product):
        value = product(lefts[0], rights[0]) + product(lefts[0], rights[1]) + product(lefts[1], rights[0])
        return (-value).astype(BF16)

    def final(of_fwd, of_bwd):
        left = reflect((rows_of[0], rows_of[1]), (of_bwd[0], of_bwd[1]), dot)
        right = reflect((cols_of[0], cols_of[1]), (of_fwd[0], of_fwd[1]), dot_first)
        for time, both, late in ((y, here, shifted), (1 - y, there, there_shifted)):
            rows = at(time, here.shape[1])
            forward[rows] = (both[0, :, mine].astype(F32) + dot_last(late[...], left)).astype(BF16)
            backward[rows] = (late[:, mine].astype(F32) + dot_last(both[0], right)).astype(BF16)

    @pl.when(core == 0)
    def _():
        final(inv, inv_core)

    @pl.when(core == 1)
    def _():
        final(inv_core, inv)


def ahead(piece, by):
    size = lax.axis_size("z")
    return lax.ppermute(piece, "z", [(i, (i + by) % size) for i in range(size)])


def exchange(pieces):
    both = [(i, 3 - i) for i in range(4)]
    return [pieces[0], swap(pieces[1], "y"), swap(pieces[2], "x"), lax.ppermute(pieces[3], ("x", "y"), both)]


def scatter_z(pieces):
    total = sum(pieces[1:], pieces[0])
    return sum((ahead(total[k], k) for k in range(1, total.shape[0])), total[0])


def z_gather(piece):
    return jnp.stack([piece] + [ahead(piece, by) for by in range(1, lax.axis_size("z"))])


def xy_gather(piece):
    return exchange([piece] * 4)


def share(rows, parts):
    return -(-rows // (8 * parts)) * 8


def local(fwd_in, bwd_in):
    y = lax.axis_index("y")
    zx = ("z", "x")
    samples, width = fwd_in.shape
    half, pair, channels = samples // 2, 2 * width, 4 * width
    depth, near_parts, parts = lax.axis_size("z"), lax.axis_size(zx), lax.axis_size(PARTS)
    pd, xd = share(3 * width, near_parts), share(2 * width, near_parts)
    po, xo = share(4 * width, parts), share(4 * width, parts)
    each = share(8 * width, parts)
    shape = jax.ShapeDtypeStruct
    square = lambda *lead: pltpu.VMEM(lead + (channels, channels), F32)
    square16 = lambda *lead: pltpu.VMEM(lead + (channels, channels), BF16)
    tables = [square(2), square16(2), square16(2)] * 2
    flat = lambda *rows: pltpu.VMEM((max(rows), LANES), F32)
    kernel = functools.partial

    own = (fwd_in, bwd_in)
    send, tail = call(
        cut_kernel,
        [shape((half, width), BF16), shape((2, 16, width), BF16)],
        [pltpu.SemaphoreType.DMA((3,))],
        0,
        *own,
        outside=2,
    )
    halo = from_behind(tail, zx)
    (front,) = call(
        front_kernel, [shape((64 + half, width), BF16)], [pltpu.SemaphoreType.DMA((3,))], 0, *own, halo, outside=2
    )
    across = [swap(send, "y"), swap(front, "y")]
    own_core = [swap(a, "core") for a in own]
    halo_core = swap(halo, "core")
    *near, back = call(
        kernel(near_kernel, width, pd, xd),
        [shape((depth, pd + xd, LANES), F32)] * 2 + [shape((2, half, width), BF16)],
        [pltpu.VMEM((samples, pair), BF16)] * 3 + [pltpu.VMEM((16, pair), BF16), flat(near_parts * pd, near_parts * xd)],
        3 * samples * pair * pair,
        *own, *own_core, halo, after(halo_core, across[0]),
    )
    near_x = swap(near[1], "x")
    across_core = [swap(across[0], "core"), swap(after(across[1], near[1]), "core")]
    here, edges, shifted, *far, tails = call(
        kernel(far_kernel, width, po, xo),
        [
            shape((2, half, channels), BF16),
            shape((2, 2, 16, channels), BF16),
            shape((half, channels), BF16),
            *[shape((depth, po + xo, LANES), F32)] * 4,
            shape((8, LANES), F32),
        ],
        [pltpu.VMEM((half, channels), BF16), flat(parts * po, parts * xo)],
        4 * half * pair * pair,
        *own, *own_core, *across, *across_core, halo, halo_core,
    )
    swapped = exchange(far)
    near_sum = scatter_z([near[0], after(near_x, swapped[1])])
    across2 = swap(after(back, swapped[1]), "y")
    far_sum = scatter_z(swapped)
    chunk = jnp.concatenate([near_sum[:pd], far_sum[:po], near_sum[pd:], far_sum[po:], tails])
    column = z_gather(chunk)
    pieces = xy_gather(after(column[:, : pd + po], across2))
    stop = NSTEPS // 2
    state = [shape((channels, channels), F32)] * 2 + [shape((8, LANES), F32)]
    full, error, iterate, scale = call(
        kernel(inverse_kernel, width, pd, po, stop),
        [shape((channels, channels), F32)] + state,
        [pltpu.VMEM((2, near_parts * pd, LANES), F32), flat(parts * po)] + tables,
        30 * channels**3,
        *pieces,
    )
    ours = jnp.stack(xy_gather(after(column[:, pd + po :], pieces[1])))
    theirs = swap(after(ours, error), "core")
    finish = lambda *args: call(
        kernel(finish_kernel, stop), [shape((2, channels, channels), BF16)], tables, 30 * channels**3, *args
    )[0]
    inv = finish(error, iterate, scale)
    refl, cross, last = call(
        kernel(reflect_kernel, width, xd, xo),
        [shape((channels, channels), BF16), shape((channels, channels), F32), shape((8, LANES), F32)],
        [pltpu.VMEM((2, near_parts * xd, LANES), F32), flat(parts * xo), square16(), square16()],
        6 * channels**3,
        ours, theirs, inv,
    )
    refl_core = swap(refl, "core")
    here2, shifted2, *packed = call(
        kernel(update_cross_kernel, each),
        [shape((2, half, channels), BF16), shape((half, channels), BF16)] + [shape((depth, each, LANES), BF16)] * 4,
        [square16(2), pltpu.VMEM((16, channels), BF16), flat(parts * each)],
        5 * half * channels * channels,
        here, shifted, edges, refl, refl_core,
    )
    across2_core = swap(across2, "core")
    full_core = swap(after(full, refl_core), "core")
    matrix2, scale2 = call(
        predict_kernel,
        [shape((channels, channels), F32), shape((8, LANES), F32)],
        [pltpu.VMEM((2, 16, channels), F32)],
        18 * channels**3,
        after(full, packed[0]), full_core, cross, refl_core, last,
    )
    error2, iterate2 = call(
        kernel(begin_kernel, stop), state[:2], tables, 30 * channels**3, matrix2, scale2
    )
    swapped = exchange(packed)
    swapped[0] = after(swapped[0], matrix2)
    wide = lambda pieces: sum((p.astype(F32) for p in pieces[1:]), pieces[0].astype(F32))
    column2 = wide(z_gather(wide(swapped).astype(BF16)))
    inv2 = finish(error2, iterate2, scale2)
    inv2_core = swap(inv2, "core")
    there2, there_shifted2 = call(
        kernel(there_kernel, width),
        [shape((2, half, channels), BF16), shape((half, channels), BF16)],
        [square16(2), pltpu.VMEM((2, half, channels), BF16), pltpu.VMEM((half, channels), BF16), pltpu.VMEM((16, channels), BF16)],
        4 * half * channels * channels,
        *own, *own_core, across2, across2_core, edges, refl, after(refl_core, column2),
    )
    ours2 = jnp.stack(xy_gather(after(column2, inv2)))
    theirs2 = swap(after(ours2, there2), "core")
    return call(
        kernel(last_kernel, width),
        [shape((samples, width), BF16)] * 2,
        [pltpu.VMEM((2, parts * each, LANES), F32), pltpu.VMEM((2, width, channels), BF16), pltpu.VMEM((2, channels, width), BF16)],
        4 * samples * channels * width,
        ours2, theirs2, inv2, inv2_core, here2, shifted2, there2, there_shifted2,
    )


def solution(mesh):
    tm, chan = mesh.shape["tm"], mesh.shape["chan"]
    split = Mesh(mesh.devices.reshape(tm // 2, 2, chan // 2, 2), ("z", "x", "y", "core"))
    spec = P(("z", "x"), ("y", "core"))
    return jax.shard_map(local, mesh=split, in_specs=(spec, spec), out_specs=(spec, spec), check_vma=False)
```

```python
import functools

import jax
import jax.numpy as jnp
from jax import lax
from jax.experimental import pallas as pl
from jax.experimental.pallas import tpu as pltpu
from jax.sharding import Mesh, PartitionSpec as P

ORDERS = 2
NSTEPS = 6
F32 = jnp.float32
BF16 = jnp.bfloat16
PARTS = ("z", "x", "y")
LANES = 128
VMEM = pl.BlockSpec(memory_space=pltpu.VMEM)


def swap(value, axis):
    return lax.ppermute(value, axis, [(0, 1), (1, 0)])


def from_behind(value, axes):
    devices = lax.axis_size(axes)
    return lax.ppermute(value, axes, [(i, i + 1) for i in range(devices - 1)])


def after(value, *others):
    return lax.optimization_barrier((value,) + others)[0]


def call(body, shapes, scratch, flops, *args, outside=0):
    size = sum(a.size * a.dtype.itemsize for a in args) + sum(s.size * s.dtype.itemsize for s in shapes)
    return pl.pallas_call(
        body,
        out_shape=shapes,
        in_specs=[pl.BlockSpec(memory_space=pltpu.HBM)] * outside + [VMEM] * (len(args) - outside),
        out_specs=[VMEM] * len(shapes),
        scratch_shapes=scratch,
        compiler_params=pltpu.CompilerParams(vmem_limit_bytes=16 << 20),
        cost_estimate=pl.CostEstimate(flops=flops, bytes_accessed=size, transcendentals=0),
    )(*args)


def dot(a, b):
    return jnp.dot(a, b, preferred_element_type=F32)


def dot_first(a, b):
    return lax.dot_general(a, b, (((0,), (0,)), ((), ())), preferred_element_type=F32)


def dot_last(a, b):
    return lax.dot_general(a, b, (((1,), (1,)), ((), ())), preferred_element_type=F32)


def halves(value):
    high = value.astype(BF16)
    return high, (value - high.astype(F32)).astype(BF16)


def thirds(value):
    high, rest = value.astype(BF16), value - value.astype(BF16).astype(F32)
    return (high,) + halves(rest)


def at(index, size):
    return pl.ds(pl.multiple_of(index * size, size), size)


def delay(source, before, out):
    rows = source.shape[0]
    step = min(rows, 256)
    top = lax.broadcasted_iota(jnp.int32, (step, 1), 0) == 0
    for r in range(0, rows, step):
        edge = (before[...] if r == 0 else source[r - 16 : r]).astype(F32)[15:16]
        moved = pltpu.roll(source[r : r + step].astype(F32), 1, 0)
        out[r : r + step] = jnp.where(top, edge, moved).astype(BF16)


def drop_end(samples, here):
    rows = samples.shape[0]

    @pl.when((lax.axis_index("core") == 1) & here)
    def _():
        tail = samples[rows - 16 :].astype(F32)
        inside = lax.broadcasted_iota(jnp.int32, (16, 1), 0) < 15
        samples[rows - 16 :] = jnp.where(inside, tail, 0.0).astype(BF16)


def emit(blocks, flat, outs, start, each, turned=True):
    used = 0
    for block in blocks:
        flat[used : used + block.shape[0]] = block
        used += block.shape[0]
    depth = outs[0].shape[0]
    parts = depth * len(outs)
    if parts * each > used:
        flat[used : parts * each] = jnp.zeros((parts * each - used, LANES), F32)
    z, x, y = lax.axis_index("z"), lax.axis_index("x"), lax.axis_index("y")
    for i, out in enumerate(outs):
        for k in range(depth):
            part = (lax.rem(z + k, depth) if turned else k) * len(outs) + ((x * 2 + y if len(outs) == 4 else x) ^ i)
            out[k, start : start + each] = flat[at(part, each)].astype(out.dtype)


def sources(depth, turned=True):
    z, x, y = lax.axis_index("z"), lax.axis_index("x"), lax.axis_index("y")
    for i in range(4):
        for k in range(depth):
            xs, ys = x ^ (i >> 1), y ^ (i & 1)
            zx = (lax.rem(z + depth - k, depth) if turned else k) * 2 + xs
            yield i, k, zx, ys


def gather_blocks(piece, depth, start, near_each, far_each, near, far):
    for i, k, zx, ys in sources(depth):
        near[ys, at(zx, near_each)] = piece(i)[k, start : start + near_each]
        far[at(zx * 2 + ys, far_each)] = piece(i)[k, start + near_each : start + near_each + far_each]


def steps(first, last, errors, highs, lows, its, ihighs, ilows, finish):
    channels = errors.shape[1]
    half = channels // 2
    top, left, right = slice(0, half), slice(0, half), slice(half, channels)
    for n in range(first, last):
        now, later = n % 2, (n + 1) % 2

        def store(table, high, low, rows, cols, value):
            if n == NSTEPS - 1:
                finish(rows, cols, value)
            else:
                table[later, rows, cols] = value
                high[later, rows, cols], low[later, rows, cols] = halves(value)

        def advance(table, high, low):
            for rows, cols in ((top, slice(0, channels)), (right, right)):
                ahigh, alow = highs[now, rows], lows[now, rows]
                bhigh, blow = high[now, :, cols], low[now, :, cols]
                value = 2.0 * table[now, rows, cols] - (dot(ahigh, bhigh) + dot(ahigh, blow) + dot(alow, bhigh))
                store(table, high, low, rows, cols, value)
                if rows == top:
                    store(table, high, low, right, left, value[:, half:].T)

        if n < NSTEPS - 1:
            advance(errors, highs, lows)
        if n >= 1:
            advance(its, ihighs, ilows)


def put(table, high, low, slot, rows, cols, value):
    table[slot, rows, cols] = value
    high[slot, rows, cols], low[slot, rows, cols] = halves(value)


def by_kind(ours, theirs, refl):
    core = lax.axis_index("core")
    refl[1 - core] = ours[...]
    refl[core] = theirs[...]


def update(both, shifted, refl, out):
    step = 256
    for r in range(0, both.shape[1], step):
        rows = slice(r, r + step)
        forward, backward = both[0, rows], shifted[rows]
        out[0, rows] = (forward.astype(F32) + dot_last(backward, refl[0])).astype(BF16)
        out[1, rows] = (backward.astype(F32) + dot_last(forward, refl[1])).astype(BF16)


def update_edge(edge, refl, out):
    late = pltpu.roll(edge[1].astype(F32), 1, 0)
    out[...] = (late + dot_last(edge[0], refl[1])).astype(BF16)


def copy_all(pairs, sems):
    copies = [pltpu.make_async_copy(source, target, sems.at[i]) for i, (source, target) in enumerate(pairs)]
    for copy in copies:
        copy.start()
    for copy in copies:
        copy.wait()


def cut_kernel(forward, backward, send, tail, sems):
    half, end = send.shape[0], forward.shape[0]
    last = pl.ds(end - 16, 16)
    pairs = [(forward.at[at(1 - lax.axis_index("y"), half)], send)]
    copy_all(pairs + [(forward.at[last], tail.at[0]), (backward.at[last], tail.at[1])], sems)


def front_kernel(forward, backward, halo, send, sems):
    half = forward.shape[0] // 2
    ahead = pl.ds(half - 16, 16)
    pairs = [
        (backward.at[at(1 - lax.axis_index("y"), half)], send.at[pl.ds(64, half)]),
        (forward.at[ahead], send.at[pl.ds(32, 16)]),
        (backward.at[ahead], send.at[pl.ds(48, 16)]),
    ]
    send[0:16], send[16:32] = halo[0], halo[1]
    copy_all(pairs, sems)


def near_kernel(width, pd, xd, forward, backward, forward_core, backward_core, halo, halo_core, *refs):
    packed, back = [refs[0].at[:, i] for i in range(2)], refs[1]
    chosen, behind, late, edge, flat = refs[2:]
    core = lax.axis_index("core")
    own, other = at(core, width), at(1 - core, width)
    rows = at(lax.axis_index("y"), back.shape[1])
    back[0], back[1] = forward[rows], backward[rows]
    behind[:, own], behind[:, other] = backward[...], backward_core[...]
    edge[:, own], edge[:, other] = halo[1], halo_core[1]

    @pl.when(core == 0)
    def _():
        chosen[:, own], chosen[:, other] = forward[...], forward_core[...]

    @pl.when(core == 1)
    def _():
        chosen[...] = behind[...]

    zx = ("z", "x")
    drop_end(chosen, lax.axis_index(zx) == lax.axis_size(zx) - 1)
    value = dot_first(chosen[...], chosen[...])
    emit([value[:width, :width], value[:width, width:], value[width:, width:]], flat, packed, 0, pd)
    delay(behind, edge, late)
    value = dot_first(forward[...], late[...])
    emit([value[:, :width], value[:, width:]], flat, packed, pd, xd)


def far_kernel(width, po, xo, *refs):
    own, across, halos = (refs[0:2], refs[2:4]), (refs[4:6], refs[6:8]), refs[8:10]
    (here, edges, shifted), packed, (tails, samples, flat) = refs[10:13], refs[13:17], refs[17:]
    y, core = lax.axis_index("y"), lax.axis_index("core")
    half = here.shape[1]
    pair = 2 * width
    rows = at(y, half)
    for c in range(2):
        mine = at(y * 2 + (core ^ c), width)
        over = at((1 - y) * 2 + (core ^ c), width)
        for kind in range(2):
            here[kind, :, mine] = own[c][kind][rows]
            here[kind, :, over] = across[c][kind][64 * kind :]
            edges[0, kind, :, mine] = halos[c][kind]
            edges[1, kind, :, mine] = own[c][kind][half - 16 : half]
            for e in range(2):
                edges[e, kind, :, over] = across[c][1][e * 32 + kind * 16 : e * 32 + kind * 16 + 16]
    samples[...] = here[core]
    drop_end(samples, lax.axis_index(PARTS) == lax.axis_size(PARTS) - 1)
    value = dot_first(samples[:, :pair], samples[:, pair:])
    blocks = lambda v: [v[i : i + width, j : j + width] for i in (0, width) for j in (0, width)]
    emit(blocks(value), flat, packed, 0, po)
    delay(here.at[1], edges.at[y, 1], shifted)
    value = dot_first(here[0, :, at(core, pair)], shifted[:, at(1 - core, pair)])
    emit(blocks(value), flat, packed, po, xo)
    for i, rows in enumerate((here[0, half - 16 :], shifted[half - 16 :])):
        row = rows.astype(F32)[15:16]
        for j in range(4):
            tails[i * 4 + j : i * 4 + j + 1] = row[:, j * LANES : (j + 1) * LANES]


def inverse_kernel(width, pd, po, stop, *refs):
    pieces, (full, error, iterate, scale), (near, far) = refs[:4], refs[4:8], refs[8:10]
    tables = refs[10:]
    errors, highs, lows, its, ihighs, ilows = tables
    gather_blocks(lambda i: pieces[i], pieces[0].shape[0], 0, pd, po, near, far)
    table = {}
    for i in range(2):
        table[2 * i, 2 * i] = lambda i=i: near[i, :width]
        table[2 * i, 2 * i + 1] = lambda i=i: near[i, width : 2 * width]
        table[2 * i + 1, 2 * i + 1] = lambda i=i: near[i, 2 * width : 3 * width]
        for j in range(2):
            table[i, 2 + j] = lambda i=i, j=j: far[(i * 2 + j) * width : (i * 2 + j + 1) * width]
    norm = jnp.zeros((8, LANES), F32)
    for (i, j), read in table.items():
        block = read()
        squares = jnp.sum((block * block).reshape(-1, 8, LANES), axis=0)
        norm = norm + (squares if i == j else 2.0 * squares)
    factor = lax.rsqrt(jnp.sum(norm, keepdims=True) + 1e-06)
    eye = lax.broadcasted_iota(jnp.int32, (width, width), 0) == lax.broadcasted_iota(jnp.int32, (width, width), 1)
    for (i, j), read in table.items():
        block = read()
        for a, b, v in ((i, j, block),) + (() if i == j else ((j, i, block.T),)):
            rows, cols = pl.ds(a * width, width), pl.ds(b * width, width)
            full[rows, cols] = v
            v = v * factor
            put(errors, highs, lows, 0, rows, cols, v)
            put(its, ihighs, ilows, 1, rows, cols, jnp.where(eye, 2.0, 0.0) - v if a == b else -v)
    scale[...] = jnp.broadcast_to(factor, scale.shape)
    steps(0, stop, *tables, None)
    error[...], iterate[...] = errors[stop % 2], its[stop % 2]


def reflect_kernel(width, xd, xo, ours, theirs, inv, out, cross, last, near, far, high, low):
    core = lax.axis_index("core")
    depth = ours.shape[1]
    for gathered, home in ((ours, core), (theirs, 1 - core)):
        gather_blocks(lambda i: gathered.at[i], depth, 0, xd, xo, near, far)
        for i in range(2):
            for j in range(2):
                places = (
                    (at(2 * i + home, width), at(2 * i + j, width), near[i, j * width : (j + 1) * width]),
                    (at(2 * home + i, width), at(2 * (1 - home) + j, width), far[(i * 2 + j) * width : (i * 2 + j + 1) * width]),
                )
                for rows, cols, value in places:
                    cross[rows, cols] = value
                    high[rows, cols], low[rows, cols] = halves(value)
    xy = lax.axis_index("x") * 2 + lax.axis_index("y")
    last[...] = ours[xy ^ 3, lax.rem(lax.axis_index("z") + 1, depth), xd + xo : xd + xo + 8]
    for chosen, product in ((0, dot_first), (1, dot)):

        @pl.when(core == chosen)
        def _():
            value = product(high[...], inv[0]) + product(high[...], inv[1]) + product(low[...], inv[0])
            out[...] = (-value).astype(BF16)


def update_cross_kernel(each, here, shifted, edges, ours, theirs, out, late, *refs):
    packed, (refl, ahead, flat) = refs[:4], refs[4:]
    by_kind(ours, theirs, refl)
    update_edge(edges.at[lax.axis_index("y")], refl, ahead)
    update(here, shifted, refl, out)
    delay(out.at[1], ahead, late)
    channels = here.shape[2]
    value = dot_first(out[0, :, at(lax.axis_index("core"), channels // 2)], late[...])
    emit([value[:, j : j + LANES] for j in range(0, channels, LANES)], flat, packed, 0, each, turned=False)


def there_kernel(width, *refs):
    own, across, (edges, ours, theirs) = (refs[0:2], refs[2:4]), refs[4:6], refs[6:9]
    out, late, refl, raw, shifted, ahead = refs[9:]
    y, core = lax.axis_index("y"), lax.axis_index("core")
    by_kind(ours, theirs, refl)
    edge = edges.at[1 - y]
    rows = at(1 - y, raw.shape[1])
    for c in range(2):
        for kind in range(2):
            raw[kind, :, at(y * 2 + (core ^ c), width)] = own[c][kind][rows]
            raw[kind, :, at((1 - y) * 2 + (core ^ c), width)] = across[c][kind]
    delay(raw.at[1], edge.at[1], shifted)
    update_edge(edge, refl, ahead)
    update(raw, shifted, refl, out)
    delay(out.at[1], ahead, late)


def predict_kernel(own, other, cross, theirs, last, work, scale, row):
    core = lax.axis_index("core")
    channels = own.shape[0]
    refl = theirs[...]
    for chosen, product in ((0, dot_last), (1, dot)):

        @pl.when(core == chosen)
        def _():
            parts = thirds(cross[...])
            work[...] = product(refl, parts[2]) + product(refl, parts[1]) + product(refl, parts[0])

    mixed = work[...]
    total = own[...] + (mixed + mixed.T)
    parts = thirds(other[...])
    parts = thirds(dot(refl, parts[2]) + dot(refl, parts[1]) + dot(refl, parts[0]))
    work[...] = total + (dot_last(parts[2], refl) + dot_last(parts[1], refl) + dot_last(parts[0], refl))

    @pl.when(core == 1)
    def _():
        row[...] = jnp.zeros_like(row)
        for i in range(2):
            for j in range(4):
                row[i, 0:1, j * LANES : (j + 1) * LANES] = last[i * 4 + j : i * 4 + j + 1]
        end = (row[1] + dot_last(row[0].astype(BF16), refl)).astype(BF16)
        work[...] -= dot_first(end, end)

    total = work[...]
    norm = jnp.sum((total * total).reshape(-1, 8, channels), axis=0)
    factor = lax.rsqrt(jnp.sum(norm, keepdims=True) + 1e-06)
    scale[...] = jnp.broadcast_to(factor, scale.shape)


def begin_kernel(stop, matrix, scale, error, iterate, *tables):
    errors, highs, lows, its, ihighs, ilows = tables
    channels = matrix.shape[0]
    factor = scale[0:1, 0:1]
    every = pl.ds(0, channels)
    step = 128
    for r in range(0, channels, step):
        rows = pl.ds(r, step)
        value = matrix[rows] * factor
        put(errors, highs, lows, 0, rows, every, value)
        shape = (step, channels)
        eye = lax.broadcasted_iota(jnp.int32, shape, 0) + r == lax.broadcasted_iota(jnp.int32, shape, 1)
        put(its, ihighs, ilows, 1, rows, every, jnp.where(eye, 2.0, 0.0) - value)
    steps(0, stop, *tables, None)
    error[...], iterate[...] = errors[stop % 2], its[stop % 2]


def finish_kernel(start, error, iterate, scale, out, *tables):
    errors, highs, lows, its, ihighs, ilows = tables
    channels = error.shape[0]
    every = pl.ds(0, channels)
    put(errors, highs, lows, start % 2, every, every, error[...])
    put(its, ihighs, ilows, start % 2, every, every, iterate[...])
    factor = scale[0:1, 0:1]

    def finish(rows, cols, value):
        out[0, rows, cols], out[1, rows, cols] = halves(value * factor)

    steps(start, NSTEPS, *tables, finish)


def last_kernel(width, ours, theirs, inv, inv_core, here, shifted, there, there_shifted, forward, backward, flat, rows_of, cols_of):
    y, core = lax.axis_index("y"), lax.axis_index("core")
    channels = here.shape[2]
    half, depth, each = channels // 2, ours.shape[1], ours.shape[2]
    for gathered, home in ((ours, core), (theirs, 1 - core)):
        for i, k, zx, ys in sources(depth, turned=False):
            flat[home, at(zx * 2 + ys, each)] = gathered[i, k]
    for n in range(channels // LANES):
        value = flat[y, at(2 * n + core, width)]
        rows_of[0, :, n * LANES : (n + 1) * LANES], rows_of[1, :, n * LANES : (n + 1) * LANES] = halves(value)
    for home in range(2):
        value = flat[home, at(y * 2 + core, half)]
        cols_of[0, home * half : (home + 1) * half], cols_of[1, home * half : (home + 1) * half] = halves(value)
    mine = at(y * 2 + core, width)

    def reflect(lefts, rights, product):
        value = product(lefts[0], rights[0]) + product(lefts[0], rights[1]) + product(lefts[1], rights[0])
        return (-value).astype(BF16)

    def final(of_fwd, of_bwd):
        left = reflect((rows_of[0], rows_of[1]), (of_bwd[0], of_bwd[1]), dot)
        right = reflect((cols_of[0], cols_of[1]), (of_fwd[0], of_fwd[1]), dot_first)
        for time, both, late in ((y, here, shifted), (1 - y, there, there_shifted)):
            rows = at(time, here.shape[1])
            forward[rows] = (both[0, :, mine].astype(F32) + dot_last(late[...], left)).astype(BF16)
            backward[rows] = (late[:, mine].astype(F32) + dot_last(both[0], right)).astype(BF16)

    @pl.when(core == 0)
    def _():
        final(inv, inv_core)

    @pl.when(core == 1)
    def _():
        final(inv_core, inv)


def ahead(piece, by):
    size = lax.axis_size("z")
    return lax.ppermute(piece, "z", [(i, (i + by) % size) for i in range(size)])


def exchange(pieces):
    both = [(i, 3 - i) for i in range(4)]
    return [pieces[0], swap(pieces[1], "y"), swap(pieces[2], "x"), lax.ppermute(pieces[3], ("x", "y"), both)]


def scatter_z(pieces):
    total = sum(pieces[1:], pieces[0])
    return sum((ahead(total[k], k) for k in range(1, total.shape[0])), total[0])


def z_gather(piece):
    return jnp.stack([piece] + [ahead(piece, by) for by in range(1, lax.axis_size("z"))])


def xy_gather(piece):
    return exchange([piece] * 4)


def share(rows, parts):
    return -(-rows // (8 * parts)) * 8


def local(fwd_in, bwd_in):
    y = lax.axis_index("y")
    zx = ("z", "x")
    samples, width = fwd_in.shape
    half, pair, channels = samples // 2, 2 * width, 4 * width
    depth, near_parts, parts = lax.axis_size("z"), lax.axis_size(zx), lax.axis_size(PARTS)
    pd, xd = share(3 * width, near_parts), share(2 * width, near_parts)
    po, xo = share(4 * width, parts), share(4 * width, parts)
    each = share(8 * width, parts)
    shape = jax.ShapeDtypeStruct
    square = lambda *lead: pltpu.VMEM(lead + (channels, channels), F32)
    square16 = lambda *lead: pltpu.VMEM(lead + (channels, channels), BF16)
    tables = [square(2), square16(2), square16(2)] * 2
    flat = lambda *rows: pltpu.VMEM((max(rows), LANES), F32)
    kernel = functools.partial

    own = (fwd_in, bwd_in)
    send, tail = call(
        cut_kernel,
        [shape((half, width), BF16), shape((2, 16, width), BF16)],
        [pltpu.SemaphoreType.DMA((3,))],
        0,
        *own,
        outside=2,
    )
    halo = from_behind(tail, zx)
    (front,) = call(
        front_kernel, [shape((64 + half, width), BF16)], [pltpu.SemaphoreType.DMA((3,))], 0, *own, halo, outside=2
    )
    across = [swap(send, "y"), swap(front, "y")]
    own_core = [swap(a, "core") for a in own]
    halo_core = swap(halo, "core")
    near, back = call(
        kernel(near_kernel, width, pd, xd),
        [shape((depth, 2, pd + xd, LANES), F32), shape((2, half, width), BF16)],
        [pltpu.VMEM((samples, pair), BF16)] * 3 + [pltpu.VMEM((16, pair), BF16), flat(near_parts * pd, near_parts * xd)],
        3 * samples * pair * pair,
        *own, *own_core, halo, after(halo_core, across[0]),
    )
    near_got = [ahead(near[k], k) for k in range(1, depth)]
    across_core = [swap(across[0], "core"), swap(after(across[1], near), "core")]
    here, edges, shifted, *far, tails = call(
        kernel(far_kernel, width, po, xo),
        [
            shape((2, half, channels), BF16),
            shape((2, 2, 16, channels), BF16),
            shape((half, channels), BF16),
            *[shape((depth, po + xo, LANES), F32)] * 4,
            shape((8, LANES), F32),
        ],
        [pltpu.VMEM((half, channels), BF16), flat(parts * po, parts * xo)],
        4 * half * pair * pair,
        *own, *own_core, *across, *across_core, halo, halo_core,
    )
    swapped = exchange(far)
    near_z = sum((after(got, *swapped[1:]) for got in near_got), near[0])
    near_sum = near_z[0] + swap(near_z[1], "x")
    across2 = swap(after(back, swapped[1]), "y")
    far_sum = scatter_z(swapped)
    chunk = jnp.concatenate([near_sum[:pd], far_sum[:po], near_sum[pd:], far_sum[po:], tails])
    column = z_gather(chunk)
    pieces = xy_gather(after(column[:, : pd + po], across2))
    stop = NSTEPS // 2
    state = [shape((channels, channels), F32)] * 2 + [shape((8, LANES), F32)]
    full, error, iterate, scale = call(
        kernel(inverse_kernel, width, pd, po, stop),
        [shape((channels, channels), F32)] + state,
        [pltpu.VMEM((2, near_parts * pd, LANES), F32), flat(parts * po)] + tables,
        30 * channels**3,
        *pieces,
    )
    ours = jnp.stack(xy_gather(after(column[:, pd + po :], pieces[1])))
    theirs = swap(after(ours, error), "core")
    finish = lambda *args: call(
        kernel(finish_kernel, stop), [shape((2, channels, channels), BF16)], tables, 30 * channels**3, *args
    )[0]
    inv = finish(error, iterate, scale)
    refl, cross, last = call(
        kernel(reflect_kernel, width, xd, xo),
        [shape((channels, channels), BF16), shape((channels, channels), F32), shape((8, LANES), F32)],
        [pltpu.VMEM((2, near_parts * xd, LANES), F32), flat(parts * xo), square16(), square16()],
        6 * channels**3,
        ours, theirs, inv,
    )
    refl_core = swap(refl, "core")
    here2, shifted2, *packed = call(
        kernel(update_cross_kernel, each),
        [shape((2, half, channels), BF16), shape((half, channels), BF16)] + [shape((depth, each, LANES), BF16)] * 4,
        [square16(2), pltpu.VMEM((16, channels), BF16), flat(parts * each)],
        5 * half * channels * channels,
        here, shifted, edges, refl, refl_core,
    )
    across2_core = swap(across2, "core")
    full_core = swap(after(full, refl_core), "core")
    matrix2, scale2 = call(
        predict_kernel,
        [shape((channels, channels), F32), shape((8, LANES), F32)],
        [pltpu.VMEM((2, 16, channels), F32)],
        18 * channels**3,
        after(full, packed[0]), full_core, cross, refl_core, last,
    )
    error2, iterate2 = call(
        kernel(begin_kernel, stop), state[:2], tables, 30 * channels**3, matrix2, scale2
    )
    swapped = exchange(packed)
    swapped[0] = after(swapped[0], matrix2)
    wide = lambda pieces: sum((p.astype(F32) for p in pieces[1:]), pieces[0].astype(F32))
    column2 = wide(z_gather(wide(swapped).astype(BF16)))
    inv2 = finish(error2, iterate2, scale2)
    inv2_core = swap(inv2, "core")
    there2, there_shifted2 = call(
        kernel(there_kernel, width),
        [shape((2, half, channels), BF16), shape((half, channels), BF16)],
        [square16(2), pltpu.VMEM((2, half, channels), BF16), pltpu.VMEM((half, channels), BF16), pltpu.VMEM((16, channels), BF16)],
        4 * half * channels * channels,
        *own, *own_core, across2, across2_core, edges, refl, after(refl_core, column2),
    )
    ours2 = jnp.stack(xy_gather(after(column2, inv2)))
    theirs2 = swap(after(ours2, there2), "core")
    return call(
        kernel(last_kernel, width),
        [shape((samples, width), BF16)] * 2,
        [pltpu.VMEM((2, parts * each, LANES), F32), pltpu.VMEM((2, width, channels), BF16), pltpu.VMEM((2, channels, width), BF16)],
        4 * samples * channels * width,
        ours2, theirs2, inv2, inv2_core, here2, shifted2, there2, there_shifted2,
    )


def solution(mesh):
    tm, chan = mesh.shape["tm"], mesh.shape["chan"]
    split = Mesh(mesh.devices.reshape(tm // 2, 2, chan // 2, 2), ("z", "x", "y", "core"))
    spec = P(("z", "x"), ("y", "core"))
    return jax.shard_map(local, mesh=split, in_specs=(spec, spec), out_specs=(spec, spec), check_vma=False)
```

```python
import functools

import jax
import jax.numpy as jnp
from jax import lax
from jax.experimental import pallas as pl
from jax.experimental.pallas import tpu as pltpu
from jax.sharding import Mesh, PartitionSpec as P

ORDERS = 2
NSTEPS = 6
F32 = jnp.float32
BF16 = jnp.bfloat16
PARTS = ("z", "x", "y")
LANES = 128
VMEM = pl.BlockSpec(memory_space=pltpu.VMEM)


def swap(value, axis):
    return lax.ppermute(value, axis, [(0, 1), (1, 0)])


def from_behind(value, axes):
    devices = lax.axis_size(axes)
    return lax.ppermute(value, axes, [(i, i + 1) for i in range(devices - 1)])


def after(value, *others):
    return lax.optimization_barrier((value,) + others)[0]


def call(body, shapes, scratch, flops, *args, outside=0):
    size = sum(a.size * a.dtype.itemsize for a in args) + sum(s.size * s.dtype.itemsize for s in shapes)
    return pl.pallas_call(
        body,
        out_shape=shapes,
        in_specs=[pl.BlockSpec(memory_space=pltpu.HBM)] * outside + [VMEM] * (len(args) - outside),
        out_specs=[VMEM] * len(shapes),
        scratch_shapes=scratch,
        compiler_params=pltpu.CompilerParams(vmem_limit_bytes=16 << 20),
        cost_estimate=pl.CostEstimate(flops=flops, bytes_accessed=size, transcendentals=0),
    )(*args)


def dot(a, b):
    return jnp.dot(a, b, preferred_element_type=F32)


def dot_first(a, b):
    return lax.dot_general(a, b, (((0,), (0,)), ((), ())), preferred_element_type=F32)


def dot_last(a, b):
    return lax.dot_general(a, b, (((1,), (1,)), ((), ())), preferred_element_type=F32)


def halves(value):
    high = value.astype(BF16)
    return high, (value - high.astype(F32)).astype(BF16)


def thirds(value):
    high, rest = value.astype(BF16), value - value.astype(BF16).astype(F32)
    return (high,) + halves(rest)


def at(index, size):
    return pl.ds(pl.multiple_of(index * size, size), size)


def delay(source, before, out):
    rows = source.shape[0]
    step = min(rows, 256)
    top = lax.broadcasted_iota(jnp.int32, (step, 1), 0) == 0
    for r in range(0, rows, step):
        edge = (before[...] if r == 0 else source[r - 16 : r]).astype(F32)[15:16]
        moved = pltpu.roll(source[r : r + step].astype(F32), 1, 0)
        out[r : r + step] = jnp.where(top, edge, moved).astype(BF16)


def drop_end(samples, here):
    rows = samples.shape[0]

    @pl.when((lax.axis_index("core") == 1) & here)
    def _():
        tail = samples[rows - 16 :].astype(F32)
        inside = lax.broadcasted_iota(jnp.int32, (16, 1), 0) < 15
        samples[rows - 16 :] = jnp.where(inside, tail, 0.0).astype(BF16)


def emit(blocks, flat, outs, start, each, turned=True):
    used = 0
    for block in blocks:
        flat[used : used + block.shape[0]] = block
        used += block.shape[0]
    depth = outs[0].shape[0]
    parts = depth * len(outs)
    if parts * each > used:
        flat[used : parts * each] = jnp.zeros((parts * each - used, LANES), F32)
    z, x, y = lax.axis_index("z"), lax.axis_index("x"), lax.axis_index("y")
    for i, out in enumerate(outs):
        for k in range(depth):
            part = (lax.rem(z + k, depth) if turned else k) * len(outs) + ((x * 2 + y if len(outs) == 4 else x) ^ i)
            out[k, start : start + each] = flat[at(part, each)].astype(out.dtype)


def sources(depth, turned=True):
    z, x, y = lax.axis_index("z"), lax.axis_index("x"), lax.axis_index("y")
    for i in range(4):
        for k in range(depth):
            xs, ys = x ^ (i >> 1), y ^ (i & 1)
            zx = (lax.rem(z + depth - k, depth) if turned else k) * 2 + xs
            yield i, k, zx, ys


def gather_blocks(piece, depth, start, near_each, far_each, near, far):
    for i, k, zx, ys in sources(depth):
        near[ys, at(zx, near_each)] = piece(i)[k, start : start + near_each]
        far[at(zx * 2 + ys, far_each)] = piece(i)[k, start + near_each : start + near_each + far_each]


def steps(first, last, errors, highs, lows, its, ihighs, ilows, finish):
    channels = errors.shape[1]
    half = channels // 2
    top, left, right = slice(0, half), slice(0, half), slice(half, channels)
    for n in range(first, last):
        now, later = n % 2, (n + 1) % 2

        def store(table, high, low, rows, cols, value):
            if n == NSTEPS - 1:
                finish(rows, cols, value)
            else:
                table[later, rows, cols] = value
                high[later, rows, cols], low[later, rows, cols] = halves(value)

        def advance(table, high, low):
            for rows, cols in ((top, slice(0, channels)), (right, right)):
                ahigh, alow = highs[now, rows], lows[now, rows]
                bhigh, blow = high[now, :, cols], low[now, :, cols]
                value = 2.0 * table[now, rows, cols] - (dot(ahigh, bhigh) + dot(ahigh, blow) + dot(alow, bhigh))
                store(table, high, low, rows, cols, value)
                if rows == top:
                    store(table, high, low, right, left, value[:, half:].T)

        if n < NSTEPS - 1:
            advance(errors, highs, lows)
        if n >= 1:
            advance(its, ihighs, ilows)


def put(table, high, low, slot, rows, cols, value):
    table[slot, rows, cols] = value
    high[slot, rows, cols], low[slot, rows, cols] = halves(value)


def by_kind(ours, theirs, refl):
    core = lax.axis_index("core")
    refl[1 - core] = ours[...]
    refl[core] = theirs[...]


def update(both, shifted, refl, out):
    step = 256
    for r in range(0, both.shape[1], step):
        rows = slice(r, r + step)
        forward, backward = both[0, rows], shifted[rows]
        out[0, rows] = (forward.astype(F32) + dot_last(backward, refl[0])).astype(BF16)
        out[1, rows] = (backward.astype(F32) + dot_last(forward, refl[1])).astype(BF16)


def update_edge(edge, refl, out):
    late = pltpu.roll(edge[1].astype(F32), 1, 0)
    out[...] = (late + dot_last(edge[0], refl[1])).astype(BF16)


def copy_all(pairs, sems):
    copies = [pltpu.make_async_copy(source, target, sems.at[i]) for i, (source, target) in enumerate(pairs)]
    for copy in copies:
        copy.start()
    for copy in copies:
        copy.wait()


def cut_kernel(forward, backward, send, tail, sems):
    half, end = send.shape[0], forward.shape[0]
    last = pl.ds(end - 16, 16)
    pairs = [(forward.at[at(1 - lax.axis_index("y"), half)], send)]
    copy_all(pairs + [(forward.at[last], tail.at[0]), (backward.at[last], tail.at[1])], sems)


def front_kernel(forward, backward, halo, send, sems):
    half = forward.shape[0] // 2
    ahead = pl.ds(half - 16, 16)
    pairs = [
        (backward.at[at(1 - lax.axis_index("y"), half)], send.at[pl.ds(64, half)]),
        (forward.at[ahead], send.at[pl.ds(32, 16)]),
        (backward.at[ahead], send.at[pl.ds(48, 16)]),
    ]
    send[0:16], send[16:32] = halo[0], halo[1]
    copy_all(pairs, sems)


def near_kernel(width, pd, xd, forward, backward, forward_core, backward_core, halo, halo_core, *refs):
    packed, back = [refs[0].at[:, i] for i in range(2)], refs[1]
    chosen, behind, late, edge, flat = refs[2:]
    core = lax.axis_index("core")
    own, other = at(core, width), at(1 - core, width)
    rows = at(lax.axis_index("y"), back.shape[1])
    back[0], back[1] = forward[rows], backward[rows]
    behind[:, own], behind[:, other] = backward[...], backward_core[...]
    edge[:, own], edge[:, other] = halo[1], halo_core[1]

    @pl.when(core == 0)
    def _():
        chosen[:, own], chosen[:, other] = forward[...], forward_core[...]

    @pl.when(core == 1)
    def _():
        chosen[...] = behind[...]

    zx = ("z", "x")
    drop_end(chosen, lax.axis_index(zx) == lax.axis_size(zx) - 1)
    value = dot_first(chosen[...], chosen[...])
    emit([value[:width, :width], value[:width, width:], value[width:, width:]], flat, packed, 0, pd)
    delay(behind, edge, late)
    value = dot_first(forward[...], late[...])
    emit([value[:, :width], value[:, width:]], flat, packed, pd, xd)


def far_kernel(width, po, xo, *refs):
    own, across, halos = (refs[0:2], refs[2:4]), (refs[4:6], refs[6:8]), refs[8:10]
    (here, edges, shifted), packed, (tails, samples, flat) = refs[10:13], refs[13:17], refs[17:]
    y, core = lax.axis_index("y"), lax.axis_index("core")
    half = here.shape[1]
    pair = 2 * width
    rows = at(y, half)
    for c in range(2):
        mine = at(y * 2 + (core ^ c), width)
        over = at((1 - y) * 2 + (core ^ c), width)
        for kind in range(2):
            here[kind, :, mine] = own[c][kind][rows]
            here[kind, :, over] = across[c][kind][64 * kind :]
            edges[0, kind, :, mine] = halos[c][kind]
            edges[1, kind, :, mine] = own[c][kind][half - 16 : half]
            for e in range(2):
                edges[e, kind, :, over] = across[c][1][e * 32 + kind * 16 : e * 32 + kind * 16 + 16]
    samples[...] = here[core]
    drop_end(samples, lax.axis_index(PARTS) == lax.axis_size(PARTS) - 1)
    value = dot_first(samples[:, :pair], samples[:, pair:])
    blocks = lambda v: [v[i : i + width, j : j + width] for i in (0, width) for j in (0, width)]
    emit(blocks(value), flat, packed, 0, po)
    delay(here.at[1], edges.at[y, 1], shifted)
    value = dot_first(here[0, :, at(core, pair)], shifted[:, at(1 - core, pair)])
    emit(blocks(value), flat, packed, po, xo)
    for i, rows in enumerate((here[0, half - 16 :], shifted[half - 16 :])):
        row = rows.astype(F32)[15:16]
        for j in range(4):
            tails[i * 4 + j : i * 4 + j + 1] = row[:, j * LANES : (j + 1) * LANES]


def inverse_kernel(width, pd, po, stop, *refs):
    pieces, (full, error, iterate, scale), (near, far) = refs[:4], refs[4:8], refs[8:10]
    tables = refs[10:]
    errors, highs, lows, its, ihighs, ilows = tables
    gather_blocks(lambda i: pieces[i], pieces[0].shape[0], 0, pd, po, near, far)
    table = {}
    for i in range(2):
        table[2 * i, 2 * i] = lambda i=i: near[i, :width]
        table[2 * i, 2 * i + 1] = lambda i=i: near[i, width : 2 * width]
        table[2 * i + 1, 2 * i + 1] = lambda i=i: near[i, 2 * width : 3 * width]
        for j in range(2):
            table[i, 2 + j] = lambda i=i, j=j: far[(i * 2 + j) * width : (i * 2 + j + 1) * width]
    norm = jnp.zeros((8, LANES), F32)
    for (i, j), read in table.items():
        block = read()
        squares = jnp.sum((block * block).reshape(-1, 8, LANES), axis=0)
        norm = norm + (squares if i == j else 2.0 * squares)
    factor = lax.rsqrt(jnp.sum(norm, keepdims=True) + 1e-06)
    eye = lax.broadcasted_iota(jnp.int32, (width, width), 0) == lax.broadcasted_iota(jnp.int32, (width, width), 1)
    for (i, j), read in table.items():
        block = read()
        for a, b, v in ((i, j, block),) + (() if i == j else ((j, i, block.T),)):
            rows, cols = pl.ds(a * width, width), pl.ds(b * width, width)
            full[rows, cols] = v
            v = v * factor
            put(errors, highs, lows, 0, rows, cols, v)
            put(its, ihighs, ilows, 1, rows, cols, jnp.where(eye, 2.0, 0.0) - v if a == b else -v)
    scale[...] = jnp.broadcast_to(factor, scale.shape)
    steps(0, stop, *tables, None)
    error[...], iterate[...] = errors[stop % 2], its[stop % 2]


def reflect_kernel(width, xd, xo, ours, theirs, inv, out, cross, last, near, far, high, low):
    core = lax.axis_index("core")
    depth = ours.shape[1]
    for gathered, home in ((ours, core), (theirs, 1 - core)):
        gather_blocks(lambda i: gathered.at[i], depth, 0, xd, xo, near, far)
        for i in range(2):
            for j in range(2):
                places = (
                    (at(2 * i + home, width), at(2 * i + j, width), near[i, j * width : (j + 1) * width]),
                    (at(2 * home + i, width), at(2 * (1 - home) + j, width), far[(i * 2 + j) * width : (i * 2 + j + 1) * width]),
                )
                for rows, cols, value in places:
                    cross[rows, cols] = value
                    high[rows, cols], low[rows, cols] = halves(value)
    xy = lax.axis_index("x") * 2 + lax.axis_index("y")
    last[...] = ours[xy ^ 3, lax.rem(lax.axis_index("z") + 1, depth), xd + xo : xd + xo + 8]
    for chosen, product in ((0, dot_first), (1, dot)):

        @pl.when(core == chosen)
        def _():
            value = product(high[...], inv[0]) + product(high[...], inv[1]) + product(low[...], inv[0])
            out[...] = (-value).astype(BF16)


def update_own_kernel(here, shifted, ours, out):
    core = lax.axis_index("core")
    for chosen, base, signal in ((0, shifted, here.at[0]), (1, here.at[0], shifted)):

        @pl.when(core == chosen)
        def _():
            for r in range(0, out.shape[0], 256):
                rows = slice(r, r + 256)
                out[rows] = (base[rows].astype(F32) + dot_last(signal[rows], ours[...])).astype(BF16)


def update_cross_kernel(each, here, shifted, done, edges, ours, theirs, out, late, *refs):
    packed, (refl, ahead, flat) = refs[:4], refs[4:]
    core = lax.axis_index("core")
    by_kind(ours, theirs, refl)
    update_edge(edges.at[lax.axis_index("y")], refl, ahead)
    out[1 - core] = done[...]
    for chosen, base, signal in ((1, shifted, here.at[0]), (0, here.at[0], shifted)):

        @pl.when(core == chosen)
        def _():
            for r in range(0, out.shape[1], 256):
                rows = slice(r, r + 256)
                out[chosen, rows] = (base[rows].astype(F32) + dot_last(signal[rows], theirs[...])).astype(BF16)

    delay(out.at[1], ahead, late)
    channels = here.shape[2]
    value = dot_first(out[0, :, at(core, channels // 2)], late[...])
    emit([value[:, j : j + LANES] for j in range(0, channels, LANES)], flat, packed, 0, each, turned=False)


def there_kernel(width, *refs):
    own, across, (edges, ours, theirs) = (refs[0:2], refs[2:4]), refs[4:6], refs[6:9]
    out, late, refl, raw, shifted, ahead = refs[9:]
    y, core = lax.axis_index("y"), lax.axis_index("core")
    by_kind(ours, theirs, refl)
    edge = edges.at[1 - y]
    rows = at(1 - y, raw.shape[1])
    for c in range(2):
        for kind in range(2):
            raw[kind, :, at(y * 2 + (core ^ c), width)] = own[c][kind][rows]
            raw[kind, :, at((1 - y) * 2 + (core ^ c), width)] = across[c][kind]
    delay(raw.at[1], edge.at[1], shifted)
    update_edge(edge, refl, ahead)
    update(raw, shifted, refl, out)
    delay(out.at[1], ahead, late)


def predict_kernel(own, other, cross, theirs, last, work, scale, row):
    core = lax.axis_index("core")
    channels = own.shape[0]
    refl = theirs[...]
    for chosen, product in ((0, dot_last), (1, dot)):

        @pl.when(core == chosen)
        def _():
            parts = thirds(cross[...])
            work[...] = product(refl, parts[2]) + product(refl, parts[1]) + product(refl, parts[0])

    mixed = work[...]
    total = own[...] + (mixed + mixed.T)
    parts = thirds(other[...])
    parts = thirds(dot(refl, parts[2]) + dot(refl, parts[1]) + dot(refl, parts[0]))
    work[...] = total + (dot_last(parts[2], refl) + dot_last(parts[1], refl) + dot_last(parts[0], refl))

    @pl.when(core == 1)
    def _():
        row[...] = jnp.zeros_like(row)
        for i in range(2):
            for j in range(4):
                row[i, 0:1, j * LANES : (j + 1) * LANES] = last[i * 4 + j : i * 4 + j + 1]
        end = (row[1] + dot_last(row[0].astype(BF16), refl)).astype(BF16)
        work[...] -= dot_first(end, end)

    total = work[...]
    norm = jnp.sum((total * total).reshape(-1, 8, channels), axis=0)
    factor = lax.rsqrt(jnp.sum(norm, keepdims=True) + 1e-06)
    scale[...] = jnp.broadcast_to(factor, scale.shape)


def second_inverse_kernel(matrix, scale, out, *tables):
    errors, highs, lows, its, ihighs, ilows = tables
    channels = matrix.shape[0]
    factor = scale[0:1, 0:1]
    every = pl.ds(0, channels)
    step = 128
    for r in range(0, channels, step):
        rows = pl.ds(r, step)
        value = matrix[rows] * factor
        put(errors, highs, lows, 0, rows, every, value)
        shape = (step, channels)
        eye = lax.broadcasted_iota(jnp.int32, shape, 0) + r == lax.broadcasted_iota(jnp.int32, shape, 1)
        put(its, ihighs, ilows, 1, rows, every, jnp.where(eye, 2.0, 0.0) - value)

    def finish(rows, cols, value):
        out[0, rows, cols], out[1, rows, cols] = halves(value * factor)

    steps(0, NSTEPS, *tables, finish)


def finish_kernel(start, error, iterate, scale, out, *tables):
    errors, highs, lows, its, ihighs, ilows = tables
    channels = error.shape[0]
    every = pl.ds(0, channels)
    put(errors, highs, lows, start % 2, every, every, error[...])
    put(its, ihighs, ilows, start % 2, every, every, iterate[...])
    factor = scale[0:1, 0:1]

    def finish(rows, cols, value):
        out[0, rows, cols], out[1, rows, cols] = halves(value * factor)

    steps(start, NSTEPS, *tables, finish)


def last_kernel(width, ours, theirs, inv, inv_core, here, shifted, there, there_shifted, forward, backward, flat, rows_of, cols_of):
    y, core = lax.axis_index("y"), lax.axis_index("core")
    channels = here.shape[2]
    half, depth, each = channels // 2, ours.shape[1], ours.shape[2]
    for gathered, home in ((ours, core), (theirs, 1 - core)):
        for i, k, zx, ys in sources(depth, turned=False):
            flat[home, at(zx * 2 + ys, each)] = gathered[i, k]
    for n in range(channels // LANES):
        value = flat[y, at(2 * n + core, width)]
        rows_of[0, :, n * LANES : (n + 1) * LANES], rows_of[1, :, n * LANES : (n + 1) * LANES] = halves(value)
    for home in range(2):
        value = flat[home, at(y * 2 + core, half)]
        cols_of[0, home * half : (home + 1) * half], cols_of[1, home * half : (home + 1) * half] = halves(value)
    mine = at(y * 2 + core, width)

    def reflect(lefts, rights, product):
        value = product(lefts[0], rights[0]) + product(lefts[0], rights[1]) + product(lefts[1], rights[0])
        return (-value).astype(BF16)

    def final(of_fwd, of_bwd):
        left = reflect((rows_of[0], rows_of[1]), (of_bwd[0], of_bwd[1]), dot)
        right = reflect((cols_of[0], cols_of[1]), (of_fwd[0], of_fwd[1]), dot_first)
        for time, both, late in ((y, here, shifted), (1 - y, there, there_shifted)):
            rows = at(time, here.shape[1])
            forward[rows] = (both[0, :, mine].astype(F32) + dot_last(late[...], left)).astype(BF16)
            backward[rows] = (late[:, mine].astype(F32) + dot_last(both[0], right)).astype(BF16)

    @pl.when(core == 0)
    def _():
        final(inv, inv_core)

    @pl.when(core == 1)
    def _():
        final(inv_core, inv)


def ahead(piece, by):
    size = lax.axis_size("z")
    return lax.ppermute(piece, "z", [(i, (i + by) % size) for i in range(size)])


def exchange(pieces):
    both = [(i, 3 - i) for i in range(4)]
    return [pieces[0], swap(pieces[1], "y"), swap(pieces[2], "x"), lax.ppermute(pieces[3], ("x", "y"), both)]


def scatter_z(pieces):
    total = sum(pieces[1:], pieces[0])
    return sum((ahead(total[k], k) for k in range(1, total.shape[0])), total[0])


def z_gather(piece):
    return jnp.stack([piece] + [ahead(piece, by) for by in range(1, lax.axis_size("z"))])


def xy_gather(piece):
    return exchange([piece] * 4)


def share(rows, parts):
    return -(-rows // (8 * parts)) * 8


def local(fwd_in, bwd_in):
    y = lax.axis_index("y")
    zx = ("z", "x")
    samples, width = fwd_in.shape
    half, pair, channels = samples // 2, 2 * width, 4 * width
    depth, near_parts, parts = lax.axis_size("z"), lax.axis_size(zx), lax.axis_size(PARTS)
    pd, xd = share(3 * width, near_parts), share(2 * width, near_parts)
    po, xo = share(4 * width, parts), share(4 * width, parts)
    each = share(8 * width, parts)
    shape = jax.ShapeDtypeStruct
    square = lambda *lead: pltpu.VMEM(lead + (channels, channels), F32)
    square16 = lambda *lead: pltpu.VMEM(lead + (channels, channels), BF16)
    tables = [square(2), square16(2), square16(2)] * 2
    flat = lambda *rows: pltpu.VMEM((max(rows), LANES), F32)
    kernel = functools.partial

    own = (fwd_in, bwd_in)
    send, tail = call(
        cut_kernel,
        [shape((half, width), BF16), shape((2, 16, width), BF16)],
        [pltpu.SemaphoreType.DMA((3,))],
        0,
        *own,
        outside=2,
    )
    halo = from_behind(tail, zx)
    (front,) = call(
        front_kernel, [shape((64 + half, width), BF16)], [pltpu.SemaphoreType.DMA((3,))], 0, *own, halo, outside=2
    )
    across = [swap(send, "y"), swap(front, "y")]
    own_core = [swap(a, "core") for a in own]
    halo_core = swap(halo, "core")
    near, back = call(
        kernel(near_kernel, width, pd, xd),
        [shape((depth, 2, pd + xd, LANES), F32), shape((2, half, width), BF16)],
        [pltpu.VMEM((samples, pair), BF16)] * 3 + [pltpu.VMEM((16, pair), BF16), flat(near_parts * pd, near_parts * xd)],
        3 * samples * pair * pair,
        *own, *own_core, halo, after(halo_core, across[0]),
    )
    near_got = [ahead(near[k], k) for k in range(1, depth)]
    across_core = [swap(across[0], "core"), swap(after(across[1], near), "core")]
    here, edges, shifted, *far, tails = call(
        kernel(far_kernel, width, po, xo),
        [
            shape((2, half, channels), BF16),
            shape((2, 2, 16, channels), BF16),
            shape((half, channels), BF16),
            *[shape((depth, po + xo, LANES), F32)] * 4,
            shape((8, LANES), F32),
        ],
        [pltpu.VMEM((half, channels), BF16), flat(parts * po, parts * xo)],
        4 * half * pair * pair,
        *own, *own_core, *across, *across_core, halo, halo_core,
    )
    swapped = exchange(far)
    near_z = sum((after(got, *swapped[1:]) for got in near_got), near[0])
    near_sum = near_z[0] + swap(near_z[1], "x")
    across2 = swap(after(back, swapped[1]), "y")
    far_sum = scatter_z(swapped)
    chunk = jnp.concatenate([near_sum[:pd], far_sum[:po], near_sum[pd:], far_sum[po:], tails])
    column = z_gather(chunk)
    pieces = xy_gather(after(column[:, : pd + po], across2))
    stop = NSTEPS // 2
    state = [shape((channels, channels), F32)] * 2 + [shape((8, LANES), F32)]
    full, error, iterate, scale = call(
        kernel(inverse_kernel, width, pd, po, stop),
        [shape((channels, channels), F32)] + state,
        [pltpu.VMEM((2, near_parts * pd, LANES), F32), flat(parts * po)] + tables,
        30 * channels**3,
        *pieces,
    )
    ours = jnp.stack(xy_gather(after(column[:, pd + po :], pieces[1])))
    theirs = swap(after(ours, error), "core")
    finish = lambda *args: call(
        kernel(finish_kernel, stop), [shape((2, channels, channels), BF16)], tables, 30 * channels**3, *args
    )[0]
    inv = finish(error, iterate, scale)
    refl, cross, last = call(
        kernel(reflect_kernel, width, xd, xo),
        [shape((channels, channels), BF16), shape((channels, channels), F32), shape((8, LANES), F32)],
        [pltpu.VMEM((2, near_parts * xd, LANES), F32), flat(parts * xo), square16(), square16()],
        6 * channels**3,
        ours, theirs, inv,
    )
    refl_core = swap(refl, "core")
    (done,) = call(
        update_own_kernel,
        [shape((half, channels), BF16)],
        [],
        2 * half * channels * channels,
        here, shifted, refl,
    )
    refl_core = after(refl_core, done)
    here2, shifted2, *packed = call(
        kernel(update_cross_kernel, each),
        [shape((2, half, channels), BF16), shape((half, channels), BF16)] + [shape((depth, each, LANES), BF16)] * 4,
        [square16(2), pltpu.VMEM((16, channels), BF16), flat(parts * each)],
        3 * half * channels * channels,
        here, shifted, done, edges, refl, refl_core,
    )
    across2_core = swap(across2, "core")
    full_core = swap(after(full, refl_core), "core")
    matrix2, scale2 = call(
        predict_kernel,
        [shape((channels, channels), F32), shape((8, LANES), F32)],
        [pltpu.VMEM((2, 16, channels), F32)],
        18 * channels**3,
        after(full, packed[0]), full_core, cross, refl_core, last,
    )
    swapped = exchange(packed)
    swapped[0] = after(swapped[0], matrix2)
    wide = lambda pieces: sum((p.astype(F32) for p in pieces[1:]), pieces[0].astype(F32))
    column2 = wide(z_gather(wide(swapped).astype(BF16)))
    (inv2,) = call(
        second_inverse_kernel, [shape((2, channels, channels), BF16)], tables, 60 * channels**3, matrix2, scale2
    )
    inv2_core = swap(inv2, "core")
    there2, there_shifted2 = call(
        kernel(there_kernel, width),
        [shape((2, half, channels), BF16), shape((half, channels), BF16)],
        [square16(2), pltpu.VMEM((2, half, channels), BF16), pltpu.VMEM((half, channels), BF16), pltpu.VMEM((16, channels), BF16)],
        4 * half * channels * channels,
        *own, *own_core, across2, across2_core, edges, refl, after(refl_core, column2),
    )
    ours2 = jnp.stack(xy_gather(after(column2, inv2)))
    theirs2 = swap(after(ours2, there2), "core")
    return call(
        kernel(last_kernel, width),
        [shape((samples, width), BF16)] * 2,
        [pltpu.VMEM((2, parts * each, LANES), F32), pltpu.VMEM((2, width, channels), BF16), pltpu.VMEM((2, channels, width), BF16)],
        4 * samples * channels * width,
        ours2, theirs2, inv2, inv2_core, here2, shifted2, there2, there_shifted2,
    )


def solution(mesh):
    tm, chan = mesh.shape["tm"], mesh.shape["chan"]
    split = Mesh(mesh.devices.reshape(tm // 2, 2, chan // 2, 2), ("z", "x", "y", "core"))
    spec = P(("z", "x"), ("y", "core"))
    return jax.shard_map(local, mesh=split, in_specs=(spec, spec), out_specs=(spec, spec), check_vma=False)
```

```python
import functools

import jax
import jax.numpy as jnp
from jax import lax
from jax.experimental import pallas as pl
from jax.experimental.pallas import tpu as pltpu
from jax.sharding import Mesh, PartitionSpec as P

ORDERS = 2
NSTEPS = 6
F32 = jnp.float32
BF16 = jnp.bfloat16
PARTS = ("z", "x", "y")
LANES = 128
VMEM = pl.BlockSpec(memory_space=pltpu.VMEM)


def swap(value, axis):
    return lax.ppermute(value, axis, [(0, 1), (1, 0)])


def from_behind(value, axes):
    devices = lax.axis_size(axes)
    return lax.ppermute(value, axes, [(i, i + 1) for i in range(devices - 1)])


def after(value, *others):
    return lax.optimization_barrier((value,) + others)[0]


def call(body, shapes, scratch, flops, *args, outside=0):
    size = sum(a.size * a.dtype.itemsize for a in args) + sum(s.size * s.dtype.itemsize for s in shapes)
    return pl.pallas_call(
        body,
        out_shape=shapes,
        in_specs=[pl.BlockSpec(memory_space=pltpu.HBM)] * outside + [VMEM] * (len(args) - outside),
        out_specs=[VMEM] * len(shapes),
        scratch_shapes=scratch,
        compiler_params=pltpu.CompilerParams(vmem_limit_bytes=16 << 20),
        cost_estimate=pl.CostEstimate(flops=flops, bytes_accessed=size, transcendentals=0),
    )(*args)


def dot(a, b):
    return jnp.dot(a, b, preferred_element_type=F32)


def dot_first(a, b):
    return lax.dot_general(a, b, (((0,), (0,)), ((), ())), preferred_element_type=F32)


def dot_last(a, b):
    return lax.dot_general(a, b, (((1,), (1,)), ((), ())), preferred_element_type=F32)


def halves(value):
    high = value.astype(BF16)
    return high, (value - high.astype(F32)).astype(BF16)


def thirds(value):
    high, rest = value.astype(BF16), value - value.astype(BF16).astype(F32)
    return (high,) + halves(rest)


def at(index, size):
    return pl.ds(pl.multiple_of(index * size, size), size)


def delay(source, before, out):
    rows = source.shape[0]
    step = min(rows, 256)
    top = lax.broadcasted_iota(jnp.int32, (step, 1), 0) == 0
    for r in range(0, rows, step):
        edge = (before[...] if r == 0 else source[r - 16 : r]).astype(F32)[15:16]
        moved = pltpu.roll(source[r : r + step].astype(F32), 1, 0)
        out[r : r + step] = jnp.where(top, edge, moved).astype(BF16)


def drop_end(samples, here):
    rows = samples.shape[0]

    @pl.when((lax.axis_index("core") == 1) & here)
    def _():
        tail = samples[rows - 16 :].astype(F32)
        inside = lax.broadcasted_iota(jnp.int32, (16, 1), 0) < 15
        samples[rows - 16 :] = jnp.where(inside, tail, 0.0).astype(BF16)


def emit(blocks, flat, outs, start, each, turned=True):
    used = 0
    for block in blocks:
        flat[used : used + block.shape[0]] = block
        used += block.shape[0]
    depth = outs[0].shape[0]
    parts = depth * len(outs)
    if parts * each > used:
        flat[used : parts * each] = jnp.zeros((parts * each - used, LANES), F32)
    z, x, y = lax.axis_index("z"), lax.axis_index("x"), lax.axis_index("y")
    for i, out in enumerate(outs):
        for k in range(depth):
            part = (lax.rem(z + k, depth) if turned else k) * len(outs) + ((x * 2 + y if len(outs) == 4 else x) ^ i)
            out[k, start : start + each] = flat[at(part, each)].astype(out.dtype)


def sources(depth, turned=True):
    z, x, y = lax.axis_index("z"), lax.axis_index("x"), lax.axis_index("y")
    for i in range(4):
        for k in range(depth):
            xs, ys = x ^ (i >> 1), y ^ (i & 1)
            zx = (lax.rem(z + depth - k, depth) if turned else k) * 2 + xs
            yield i, k, zx, ys


def gather_blocks(piece, depth, start, near_each, far_each, near, far):
    for i, k, zx, ys in sources(depth):
        near[ys, at(zx, near_each)] = piece(i)[k, start : start + near_each]
        far[at(zx * 2 + ys, far_each)] = piece(i)[k, start + near_each : start + near_each + far_each]


def steps(first, last, errors, highs, lows, its, ihighs, ilows, finish):
    channels = errors.shape[1]
    half = channels // 2
    top, left, right = slice(0, half), slice(0, half), slice(half, channels)
    for n in range(first, last):
        now, later = n % 2, (n + 1) % 2

        def store(table, high, low, rows, cols, value):
            if n == NSTEPS - 1:
                finish(rows, cols, value)
            else:
                table[later, rows, cols] = value
                high[later, rows, cols], low[later, rows, cols] = halves(value)

        def advance(table, high, low):
            for rows, cols in ((top, slice(0, channels)), (right, right)):
                ahigh, alow = highs[now, rows], lows[now, rows]
                bhigh, blow = high[now, :, cols], low[now, :, cols]
                left_side = jnp.concatenate([ahigh, ahigh, alow], axis=1)
                value = 2.0 * table[now, rows, cols] - dot(left_side, jnp.concatenate([bhigh, blow, bhigh], axis=0))
                store(table, high, low, rows, cols, value)
                if rows == top:
                    store(table, high, low, right, left, value[:, half:].T)

        if n < NSTEPS - 1:
            advance(errors, highs, lows)
        if n >= 1:
            advance(its, ihighs, ilows)


def put(table, high, low, slot, rows, cols, value):
    table[slot, rows, cols] = value
    high[slot, rows, cols], low[slot, rows, cols] = halves(value)


def by_kind(ours, theirs, refl):
    core = lax.axis_index("core")
    refl[1 - core] = ours[...]
    refl[core] = theirs[...]


def update(both, shifted, refl, out):
    step = 256
    for r in range(0, both.shape[1], step):
        rows = slice(r, r + step)
        forward, backward = both[0, rows], shifted[rows]
        out[0, rows] = (forward.astype(F32) + dot_last(backward, refl[0])).astype(BF16)
        out[1, rows] = (backward.astype(F32) + dot_last(forward, refl[1])).astype(BF16)


def update_edge(edge, refl, out):
    late = pltpu.roll(edge[1].astype(F32), 1, 0)
    out[...] = (late + dot_last(edge[0], refl[1])).astype(BF16)


def copy_all(pairs, sems):
    copies = [pltpu.make_async_copy(source, target, sems.at[i]) for i, (source, target) in enumerate(pairs)]
    for copy in copies:
        copy.start()
    for copy in copies:
        copy.wait()


def cut_kernel(forward, backward, send, tail, sems):
    half, end = send.shape[0], forward.shape[0]
    last = pl.ds(end - 16, 16)
    pairs = [(forward.at[at(1 - lax.axis_index("y"), half)], send)]
    copy_all(pairs + [(forward.at[last], tail.at[0]), (backward.at[last], tail.at[1])], sems)


def front_kernel(forward, backward, halo, send, sems):
    half = forward.shape[0] // 2
    ahead = pl.ds(half - 16, 16)
    pairs = [
        (backward.at[at(1 - lax.axis_index("y"), half)], send.at[pl.ds(64, half)]),
        (forward.at[ahead], send.at[pl.ds(32, 16)]),
        (backward.at[ahead], send.at[pl.ds(48, 16)]),
    ]
    send[0:16], send[16:32] = halo[0], halo[1]
    copy_all(pairs, sems)


def near_kernel(width, pd, xd, forward, backward, forward_core, backward_core, halo, halo_core, *refs):
    packed, back = [refs[0].at[:, i] for i in range(2)], refs[1]
    chosen, behind, late, edge, flat = refs[2:]
    core = lax.axis_index("core")
    own, other = at(core, width), at(1 - core, width)
    rows = at(lax.axis_index("y"), back.shape[1])
    back[0], back[1] = forward[rows], backward[rows]
    behind[:, own], behind[:, other] = backward[...], backward_core[...]
    edge[:, own], edge[:, other] = halo[1], halo_core[1]

    @pl.when(core == 0)
    def _():
        chosen[:, own], chosen[:, other] = forward[...], forward_core[...]

    @pl.when(core == 1)
    def _():
        chosen[...] = behind[...]

    zx = ("z", "x")
    drop_end(chosen, lax.axis_index(zx) == lax.axis_size(zx) - 1)
    value = dot_first(chosen[...], chosen[...])
    emit([value[:width, :width], value[:width, width:], value[width:, width:]], flat, packed, 0, pd)
    delay(behind, edge, late)
    value = dot_first(forward[...], late[...])
    emit([value[:, :width], value[:, width:]], flat, packed, pd, xd)


def far_kernel(width, po, xo, *refs):
    own, across, halos = (refs[0:2], refs[2:4]), (refs[4:6], refs[6:8]), refs[8:10]
    (here, edges, shifted), packed, (tails, samples, flat) = refs[10:13], refs[13:17], refs[17:]
    y, core = lax.axis_index("y"), lax.axis_index("core")
    half = here.shape[1]
    pair = 2 * width
    rows = at(y, half)
    for c in range(2):
        mine = at(y * 2 + (core ^ c), width)
        over = at((1 - y) * 2 + (core ^ c), width)
        for kind in range(2):
            here[kind, :, mine] = own[c][kind][rows]
            here[kind, :, over] = across[c][kind][64 * kind :]
            edges[0, kind, :, mine] = halos[c][kind]
            edges[1, kind, :, mine] = own[c][kind][half - 16 : half]
            for e in range(2):
                edges[e, kind, :, over] = across[c][1][e * 32 + kind * 16 : e * 32 + kind * 16 + 16]
    samples[...] = here[core]
    drop_end(samples, lax.axis_index(PARTS) == lax.axis_size(PARTS) - 1)
    value = dot_first(samples[:, :pair], samples[:, pair:])
    blocks = lambda v: [v[i : i + width, j : j + width] for i in (0, width) for j in (0, width)]
    emit(blocks(value), flat, packed, 0, po)
    delay(here.at[1], edges.at[y, 1], shifted)
    value = dot_first(here[0, :, at(core, pair)], shifted[:, at(1 - core, pair)])
    emit(blocks(value), flat, packed, po, xo)
    for i, rows in enumerate((here[0, half - 16 :], shifted[half - 16 :])):
        row = rows.astype(F32)[15:16]
        for j in range(4):
            tails[i * 4 + j : i * 4 + j + 1] = row[:, j * LANES : (j + 1) * LANES]


def inverse_kernel(width, pd, po, stop, *refs):
    pieces, (full, error, iterate, scale), (near, far) = refs[:4], refs[4:8], refs[8:10]
    tables = refs[10:]
    errors, highs, lows, its, ihighs, ilows = tables
    gather_blocks(lambda i: pieces[i], pieces[0].shape[0], 0, pd, po, near, far)
    table = {}
    for i in range(2):
        table[2 * i, 2 * i] = lambda i=i: near[i, :width]
        table[2 * i, 2 * i + 1] = lambda i=i: near[i, width : 2 * width]
        table[2 * i + 1, 2 * i + 1] = lambda i=i: near[i, 2 * width : 3 * width]
        for j in range(2):
            table[i, 2 + j] = lambda i=i, j=j: far[(i * 2 + j) * width : (i * 2 + j + 1) * width]
    norm = jnp.zeros((8, LANES), F32)
    for (i, j), read in table.items():
        block = read()
        squares = jnp.sum((block * block).reshape(-1, 8, LANES), axis=0)
        norm = norm + (squares if i == j else 2.0 * squares)
    factor = lax.rsqrt(jnp.sum(norm, keepdims=True) + 1e-06)
    eye = lax.broadcasted_iota(jnp.int32, (width, width), 0) == lax.broadcasted_iota(jnp.int32, (width, width), 1)
    for (i, j), read in table.items():
        block = read()
        for a, b, v in ((i, j, block),) + (() if i == j else ((j, i, block.T),)):
            rows, cols = pl.ds(a * width, width), pl.ds(b * width, width)
            full[rows, cols] = v
            v = v * factor
            put(errors, highs, lows, 0, rows, cols, v)
            put(its, ihighs, ilows, 1, rows, cols, jnp.where(eye, 2.0, 0.0) - v if a == b else -v)
    scale[...] = jnp.broadcast_to(factor, scale.shape)
    steps(0, stop, *tables, None)
    error[...], iterate[...] = errors[stop % 2], its[stop % 2]


def reflect_kernel(width, xd, xo, ours, theirs, inv, out, cross, last, near, far, high, low):
    core = lax.axis_index("core")
    depth = ours.shape[1]
    for gathered, home in ((ours, core), (theirs, 1 - core)):
        gather_blocks(lambda i: gathered.at[i], depth, 0, xd, xo, near, far)
        for i in range(2):
            for j in range(2):
                places = (
                    (at(2 * i + home, width), at(2 * i + j, width), near[i, j * width : (j + 1) * width]),
                    (at(2 * home + i, width), at(2 * (1 - home) + j, width), far[(i * 2 + j) * width : (i * 2 + j + 1) * width]),
                )
                for rows, cols, value in places:
                    cross[rows, cols] = value
                    high[rows, cols], low[rows, cols] = halves(value)
    xy = lax.axis_index("x") * 2 + lax.axis_index("y")
    last[...] = ours[xy ^ 3, lax.rem(lax.axis_index("z") + 1, depth), xd + xo : xd + xo + 8]
    for chosen, product in ((0, dot_first), (1, dot)):

        @pl.when(core == chosen)
        def _():
            value = product(high[...], inv[0]) + product(high[...], inv[1]) + product(low[...], inv[0])
            out[...] = (-value).astype(BF16)


def update_own_kernel(here, shifted, ours, out):
    core = lax.axis_index("core")
    for chosen, base, signal in ((0, shifted, here.at[0]), (1, here.at[0], shifted)):

        @pl.when(core == chosen)
        def _():
            for r in range(0, out.shape[0], 256):
                rows = slice(r, r + 256)
                out[rows] = (base[rows].astype(F32) + dot_last(signal[rows], ours[...])).astype(BF16)


def update_cross_kernel(each, here, shifted, done, edges, ours, theirs, out, late, *refs):
    packed, (refl, ahead, flat) = refs[:4], refs[4:]
    core = lax.axis_index("core")
    by_kind(ours, theirs, refl)
    update_edge(edges.at[lax.axis_index("y")], refl, ahead)
    out[1 - core] = done[...]
    for chosen, base, signal in ((1, shifted, here.at[0]), (0, here.at[0], shifted)):

        @pl.when(core == chosen)
        def _():
            for r in range(0, out.shape[1], 256):
                rows = slice(r, r + 256)
                out[chosen, rows] = (base[rows].astype(F32) + dot_last(signal[rows], theirs[...])).astype(BF16)

    delay(out.at[1], ahead, late)
    channels = here.shape[2]
    value = dot_first(out[0, :, at(core, channels // 2)], late[...])
    emit([value[:, j : j + LANES] for j in range(0, channels, LANES)], flat, packed, 0, each, turned=False)


def there_kernel(width, *refs):
    own, across, (edges, ours, theirs) = (refs[0:2], refs[2:4]), refs[4:6], refs[6:9]
    out, late, refl, raw, shifted, ahead = refs[9:]
    y, core = lax.axis_index("y"), lax.axis_index("core")
    by_kind(ours, theirs, refl)
    edge = edges.at[1 - y]
    rows = at(1 - y, raw.shape[1])
    for c in range(2):
        for kind in range(2):
            raw[kind, :, at(y * 2 + (core ^ c), width)] = own[c][kind][rows]
            raw[kind, :, at((1 - y) * 2 + (core ^ c), width)] = across[c][kind]
    delay(raw.at[1], edge.at[1], shifted)
    update_edge(edge, refl, ahead)
    update(raw, shifted, refl, out)
    delay(out.at[1], ahead, late)


def predict_kernel(own, other, cross, theirs, last, work, scale, row):
    core = lax.axis_index("core")
    channels = own.shape[0]
    refl = theirs[...]
    for chosen, product in ((0, dot_last), (1, dot)):

        @pl.when(core == chosen)
        def _():
            parts = thirds(cross[...])
            work[...] = product(refl, parts[2]) + product(refl, parts[1]) + product(refl, parts[0])

    mixed = work[...]
    total = own[...] + (mixed + mixed.T)
    parts = thirds(other[...])
    parts = thirds(dot(refl, parts[2]) + dot(refl, parts[1]) + dot(refl, parts[0]))
    work[...] = total + (dot_last(parts[2], refl) + dot_last(parts[1], refl) + dot_last(parts[0], refl))

    @pl.when(core == 1)
    def _():
        row[...] = jnp.zeros_like(row)
        for i in range(2):
            for j in range(4):
                row[i, 0:1, j * LANES : (j + 1) * LANES] = last[i * 4 + j : i * 4 + j + 1]
        end = (row[1] + dot_last(row[0].astype(BF16), refl)).astype(BF16)
        work[...] -= dot_first(end, end)

    total = work[...]
    norm = jnp.sum((total * total).reshape(-1, 8, channels), axis=0)
    factor = lax.rsqrt(jnp.sum(norm, keepdims=True) + 1e-06)
    scale[...] = jnp.broadcast_to(factor, scale.shape)


def second_inverse_kernel(matrix, scale, out, *tables):
    errors, highs, lows, its, ihighs, ilows = tables
    channels = matrix.shape[0]
    factor = scale[0:1, 0:1]
    every = pl.ds(0, channels)
    step = 128
    for r in range(0, channels, step):
        rows = pl.ds(r, step)
        value = matrix[rows] * factor
        put(errors, highs, lows, 0, rows, every, value)
        shape = (step, channels)
        eye = lax.broadcasted_iota(jnp.int32, shape, 0) + r == lax.broadcasted_iota(jnp.int32, shape, 1)
        put(its, ihighs, ilows, 1, rows, every, jnp.where(eye, 2.0, 0.0) - value)

    def finish(rows, cols, value):
        out[0, rows, cols], out[1, rows, cols] = halves(value * factor)

    steps(0, NSTEPS, *tables, finish)


def finish_kernel(start, error, iterate, scale, out, *tables):
    errors, highs, lows, its, ihighs, ilows = tables
    channels = error.shape[0]
    every = pl.ds(0, channels)
    put(errors, highs, lows, start % 2, every, every, error[...])
    put(its, ihighs, ilows, start % 2, every, every, iterate[...])
    factor = scale[0:1, 0:1]

    def finish(rows, cols, value):
        out[0, rows, cols], out[1, rows, cols] = halves(value * factor)

    steps(start, NSTEPS, *tables, finish)


def last_kernel(width, ours, theirs, inv, inv_core, here, shifted, there, there_shifted, forward, backward, flat, rows_of, cols_of):
    y, core = lax.axis_index("y"), lax.axis_index("core")
    channels = here.shape[2]
    half, depth, each = channels // 2, ours.shape[1], ours.shape[2]
    for gathered, home in ((ours, core), (theirs, 1 - core)):
        for i, k, zx, ys in sources(depth, turned=False):
            flat[home, at(zx * 2 + ys, each)] = gathered[i, k]
    for n in range(channels // LANES):
        value = flat[y, at(2 * n + core, width)]
        rows_of[0, :, n * LANES : (n + 1) * LANES], rows_of[1, :, n * LANES : (n + 1) * LANES] = halves(value)
    for home in range(2):
        value = flat[home, at(y * 2 + core, half)]
        cols_of[0, home * half : (home + 1) * half], cols_of[1, home * half : (home + 1) * half] = halves(value)
    mine = at(y * 2 + core, width)

    def reflect(lefts, rights, product):
        value = product(lefts[0], rights[0]) + product(lefts[0], rights[1]) + product(lefts[1], rights[0])
        return (-value).astype(BF16)

    def final(of_fwd, of_bwd):
        left = reflect((rows_of[0], rows_of[1]), (of_bwd[0], of_bwd[1]), dot)
        right = reflect((cols_of[0], cols_of[1]), (of_fwd[0], of_fwd[1]), dot_first)
        for time, both, late in ((y, here, shifted), (1 - y, there, there_shifted)):
            rows = at(time, here.shape[1])
            forward[rows] = (both[0, :, mine].astype(F32) + dot_last(late[...], left)).astype(BF16)
            backward[rows] = (late[:, mine].astype(F32) + dot_last(both[0], right)).astype(BF16)

    @pl.when(core == 0)
    def _():
        final(inv, inv_core)

    @pl.when(core == 1)
    def _():
        final(inv_core, inv)


def ahead(piece, by):
    size = lax.axis_size("z")
    return lax.ppermute(piece, "z", [(i, (i + by) % size) for i in range(size)])


def exchange(pieces):
    both = [(i, 3 - i) for i in range(4)]
    return [pieces[0], swap(pieces[1], "y"), swap(pieces[2], "x"), lax.ppermute(pieces[3], ("x", "y"), both)]


def scatter_z(pieces):
    total = sum(pieces[1:], pieces[0])
    return sum((ahead(total[k], k) for k in range(1, total.shape[0])), total[0])


def z_gather(piece):
    return jnp.stack([piece] + [ahead(piece, by) for by in range(1, lax.axis_size("z"))])


def xy_gather(piece):
    return exchange([piece] * 4)


def share(rows, parts):
    return -(-rows // (8 * parts)) * 8


def local(fwd_in, bwd_in):
    y = lax.axis_index("y")
    zx = ("z", "x")
    samples, width = fwd_in.shape
    half, pair, channels = samples // 2, 2 * width, 4 * width
    depth, near_parts, parts = lax.axis_size("z"), lax.axis_size(zx), lax.axis_size(PARTS)
    pd, xd = share(3 * width, near_parts), share(2 * width, near_parts)
    po, xo = share(4 * width, parts), share(4 * width, parts)
    each = share(8 * width, parts)
    shape = jax.ShapeDtypeStruct
    square = lambda *lead: pltpu.VMEM(lead + (channels, channels), F32)
    square16 = lambda *lead: pltpu.VMEM(lead + (channels, channels), BF16)
    tables = [square(2), square16(2), square16(2)] * 2
    flat = lambda *rows: pltpu.VMEM((max(rows), LANES), F32)
    kernel = functools.partial

    own = (fwd_in, bwd_in)
    send, tail = call(
        cut_kernel,
        [shape((half, width), BF16), shape((2, 16, width), BF16)],
        [pltpu.SemaphoreType.DMA((3,))],
        0,
        *own,
        outside=2,
    )
    halo = from_behind(tail, zx)
    (front,) = call(
        front_kernel, [shape((64 + half, width), BF16)], [pltpu.SemaphoreType.DMA((3,))], 0, *own, halo, outside=2
    )
    across = [swap(send, "y"), swap(front, "y")]
    own_core = [swap(a, "core") for a in own]
    halo_core = swap(halo, "core")
    near, back = call(
        kernel(near_kernel, width, pd, xd),
        [shape((depth, 2, pd + xd, LANES), F32), shape((2, half, width), BF16)],
        [pltpu.VMEM((samples, pair), BF16)] * 3 + [pltpu.VMEM((16, pair), BF16), flat(near_parts * pd, near_parts * xd)],
        3 * samples * pair * pair,
        *own, *own_core, halo, after(halo_core, across[0]),
    )
    near_got = [ahead(near[k], k) for k in range(1, depth)]
    across_core = [swap(across[0], "core"), swap(after(across[1], near), "core")]
    here, edges, shifted, *far, tails = call(
        kernel(far_kernel, width, po, xo),
        [
            shape((2, half, channels), BF16),
            shape((2, 2, 16, channels), BF16),
            shape((half, channels), BF16),
            *[shape((depth, po + xo, LANES), F32)] * 4,
            shape((8, LANES), F32),
        ],
        [pltpu.VMEM((half, channels), BF16), flat(parts * po, parts * xo)],
        4 * half * pair * pair,
        *own, *own_core, *across, *across_core, halo, halo_core,
    )
    swapped = exchange(far)
    near_z = sum((after(got, *swapped[1:]) for got in near_got), near[0])
    near_sum = near_z[0] + swap(near_z[1], "x")
    across2 = swap(after(back, swapped[1]), "y")
    far_sum = scatter_z(swapped)
    chunk = jnp.concatenate([near_sum[:pd], far_sum[:po], near_sum[pd:], far_sum[po:], tails])
    column = z_gather(chunk)
    pieces = xy_gather(after(column[:, : pd + po], across2))
    stop = NSTEPS // 2
    state = [shape((channels, channels), F32)] * 2 + [shape((8, LANES), F32)]
    full, error, iterate, scale = call(
        kernel(inverse_kernel, width, pd, po, stop),
        [shape((channels, channels), F32)] + state,
        [pltpu.VMEM((2, near_parts * pd, LANES), F32), flat(parts * po)] + tables,
        30 * channels**3,
        *pieces,
    )
    ours = jnp.stack(xy_gather(after(column[:, pd + po :], pieces[1])))
    theirs = swap(after(ours, error), "core")
    finish = lambda *args: call(
        kernel(finish_kernel, stop), [shape((2, channels, channels), BF16)], tables, 30 * channels**3, *args
    )[0]
    inv = finish(error, iterate, scale)
    refl, cross, last = call(
        kernel(reflect_kernel, width, xd, xo),
        [shape((channels, channels), BF16), shape((channels, channels), F32), shape((8, LANES), F32)],
        [pltpu.VMEM((2, near_parts * xd, LANES), F32), flat(parts * xo), square16(), square16()],
        6 * channels**3,
        ours, theirs, inv,
    )
    refl_core = swap(refl, "core")
    (done,) = call(
        update_own_kernel,
        [shape((half, channels), BF16)],
        [],
        2 * half * channels * channels,
        here, shifted, refl,
    )
    refl_core = after(refl_core, done)
    here2, shifted2, *packed = call(
        kernel(update_cross_kernel, each),
        [shape((2, half, channels), BF16), shape((half, channels), BF16)] + [shape((depth, each, LANES), BF16)] * 4,
        [square16(2), pltpu.VMEM((16, channels), BF16), flat(parts * each)],
        3 * half * channels * channels,
        here, shifted, done, edges, refl, refl_core,
    )
    across2_core = swap(across2, "core")
    full_core = swap(after(full, refl_core), "core")
    matrix2, scale2 = call(
        predict_kernel,
        [shape((channels, channels), F32), shape((8, LANES), F32)],
        [pltpu.VMEM((2, 16, channels), F32)],
        18 * channels**3,
        after(full, packed[0]), full_core, cross, refl_core, last,
    )
    swapped = exchange(packed)
    swapped[0] = after(swapped[0], matrix2)
    wide = lambda pieces: sum((p.astype(F32) for p in pieces[1:]), pieces[0].astype(F32))
    column2 = wide(z_gather(wide(swapped).astype(BF16)))
    (inv2,) = call(
        second_inverse_kernel, [shape((2, channels, channels), BF16)], tables, 60 * channels**3, matrix2, scale2
    )
    inv2_core = swap(inv2, "core")
    there2, there_shifted2 = call(
        kernel(there_kernel, width),
        [shape((2, half, channels), BF16), shape((half, channels), BF16)],
        [square16(2), pltpu.VMEM((2, half, channels), BF16), pltpu.VMEM((half, channels), BF16), pltpu.VMEM((16, channels), BF16)],
        4 * half * channels * channels,
        *own, *own_core, across2, across2_core, edges, refl, after(refl_core, column2),
    )
    ours2 = jnp.stack(xy_gather(after(column2, inv2)))
    theirs2 = swap(after(ours2, there2), "core")
    return call(
        kernel(last_kernel, width),
        [shape((samples, width), BF16)] * 2,
        [pltpu.VMEM((2, parts * each, LANES), F32), pltpu.VMEM((2, width, channels), BF16), pltpu.VMEM((2, channels, width), BF16)],
        4 * samples * channels * width,
        ours2, theirs2, inv2, inv2_core, here2, shifted2, there2, there_shifted2,
    )


def solution(mesh):
    tm, chan = mesh.shape["tm"], mesh.shape["chan"]
    split = Mesh(mesh.devices.reshape(tm // 2, 2, chan // 2, 2), ("z", "x", "y", "core"))
    spec = P(("z", "x"), ("y", "core"))
    return jax.shard_map(local, mesh=split, in_specs=(spec, spec), out_specs=(spec, spec), check_vma=False)
```
